32 devices in a mesh: gx: 8 (over y, x, core), gy: 4 (over z).
Axes of the slice: x: 2, y: 2, z: 4, core: 2. Of those that a mesh axis runs over, the one named last changes fastest.
Arguments:
- estimate: float32 [2, 1024, 512], P(None, 'gx', 'gy'), may hold values from 0.24 to 5.3
- views: bfloat16 [4, 2, 1024, 512], P(None, None, 'gx', 'gy'), may hold values from 0.18 to 7
- psf_rows: float32 [4, 31], replicated, may hold values from 0.05 to 1
- psf_cols: float32 [4, 31], replicated, may hold values from 0.05 to 1
- shifts: int32 [4, 128], P(None, 'gx'), may hold values from 0 to 3, as said below
- codes: int32 [4, 128, 4], P(None, 'gx', 'gy'), may hold values from 0 to 15
Outputs:
- updated: float32 [2, 1024, 512], P(None, 'gx', 'gy')
The draws below stay inside these ranges and needn't reach their ends.
Inputs may be any that keep to these rules, and one draw needn't show every extreme that they name: `shifts`: within each view and each group of 16 consecutive block rows that starts at a multiple of 16, no displacement occurs more than 5 times, and one occurs exactly 5 times.
All inputs are finite; a program needn't handle non-finite values.
Results may differ from the reference program's by a relative error of at most 0.0003.
Values sent between devices are 32-bit elements; how exact they have to be, the bound alone decides.
A program may use at most 64 MiB of HBM per device.

```python
import math
import jax
import jax.numpy as jnp
from jax import lax

Z = 2
TR = 128
TW = 128
BR = 8
V = 4
TAPS = 31
ITERS = 2
NBR = 128
NR = 1024
NC = 512
N_GY = 4


def banded_field(key, count, lowest, highest, planes, rows, cols):
    period_key, angle_key, phase_key, drift_key, height_key, sign_key = jax.random.split(key, 6)
    periods = jnp.exp(jax.random.uniform(period_key, (count,), jnp.float32, math.log(20.0), math.log(120.0)))
    angles = jax.random.uniform(angle_key, (count,), jnp.float32, 0.0, 2.0 * math.pi)
    phases = jax.random.uniform(phase_key, (count,), jnp.float32, 0.0, 2.0 * math.pi)
    drifts = jax.random.uniform(drift_key, (count,), jnp.float32, -0.4, 0.4)
    heights = jax.random.uniform(height_key, (count,), jnp.float32, lowest, highest)
    signs = jnp.where(jax.random.bernoulli(sign_key, 0.5, (count,)), 1.0, -1.0).astype(jnp.float32)
    plane_pos = jnp.arange(planes, dtype=jnp.float32)[:, None, None]
    row_pos = jnp.arange(rows, dtype=jnp.float32)[None, :, None]
    col_pos = jnp.arange(cols, dtype=jnp.float32)[None, None, :]
    total = jnp.zeros((planes, rows, cols), jnp.float32)
    for index in range(count):
        phase_arg = (row_pos * jnp.cos(angles[index]) + col_pos * jnp.sin(angles[index])) * (2.0 * math.pi / periods[index])
        phase_arg = phase_arg + phases[index] + drifts[index] * plane_pos
        total = total + signs[index] * heights[index] * jnp.tanh(5.0 * jnp.sin(phase_arg))
    return total


def draw_shifts(key, part):
    key = jax.random.fold_in(key, 7)
    groups = NC // TW
    tile_count = NR // TR
    blocks = TR // BR
    subkeys = jax.random.split(key, V * tile_count)
    pattern = jnp.concatenate([jnp.zeros((1,), jnp.int32), jnp.arange(blocks - 1, dtype=jnp.int32)]) % groups

    def draw_group(subkey):
        first_key, second_key = jax.random.split(subkey)
        column_order = jax.random.permutation(first_key, groups).astype(jnp.int32)
        slot_order = jax.random.permutation(second_key, blocks).astype(jnp.int32)
        return column_order[pattern[slot_order]]
    return jax.vmap(draw_group)(subkeys).reshape(V, tile_count * blocks).astype(jnp.int32)


def draw_estimate(key, part):
    shared = banded_field(key, 3, 0.2, 0.35, Z, NR, NC)
    key = jax.random.fold_in(key, 11)
    noise_key = jax.random.fold_in(key, 0)
    rough = jax.random.uniform(noise_key, (Z, NR, NC), jnp.float32, -0.35, 0.35)
    return jnp.exp(shared + rough).astype(jnp.float32)


def draw_views(key, part):
    shared = banded_field(key, 3, 0.2, 0.35, Z, NR, NC)
    key = jax.random.fold_in(key, 13)
    layers = []
    for view_id in range(V):
        view_key = jax.random.fold_in(key, view_id)
        own_key, noise_key = jax.random.split(view_key, 2)
        own = banded_field(own_key, 2, 0.2, 0.35, Z, NR, NC)
        rough = jax.random.uniform(noise_key, (Z, NR, NC), jnp.float32, -0.35, 0.35)
        layers.append(jnp.exp(0.6 * shared + own + rough))
    return jnp.stack(layers).astype(jnp.bfloat16)


def with_ends(drawn, rng, low, high):
    spot = [jax.random.randint(jax.random.fold_in(rng, axis), (), 0, length) for axis, length in enumerate(drawn.shape)]
    widest = drawn.shape.index(max(drawn.shape))
    next_to = spot[:widest] + [(spot[widest] + 1) % drawn.shape[widest]] + spot[widest + 1:]
    return drawn.at[tuple(spot)].set(low).at[tuple(next_to)].set(high)


def setup_inputs(seed: int = 0) -> dict:
    streams_of = jax.random.split(jax.random.key(seed), 7)
    estimate = draw_estimate(jax.random.fold_in(streams_of[6], 71), 0)
    views = draw_views(jax.random.fold_in(streams_of[6], 71), 0)
    psf_rows = jnp.clip(jnp.exp(jax.random.uniform(streams_of[2], (V, TAPS), jnp.float32, math.log(0.05), math.log(1.0))), 0.05, 1.0)
    psf_cols = jnp.clip(jnp.exp(jax.random.uniform(streams_of[3], (V, TAPS), jnp.float32, math.log(0.05), math.log(1.0))), 0.05, 1.0)
    shifts = draw_shifts(jax.random.fold_in(streams_of[6], 71), 0)
    codes = with_ends(jax.random.randint(streams_of[5], (V, NBR, N_GY), 0, 16), jax.random.fold_in(streams_of[5], 1), 0, 15).astype(jnp.int32)
    return {"estimate": estimate, "views": views, "psf_rows": psf_rows, "psf_cols": psf_cols, "shifts": shifts, "codes": codes}


def shift_in(values, fraction):
    last = values.shape[-1] - 1
    column = lax.broadcasted_iota(jnp.int32, values.shape, values.ndim - 1)
    following = jnp.concatenate([values[..., 1:], values[..., -1:]], axis=-1)
    return jnp.where(column < last, (1.0 - fraction) * values + fraction * following, values)


def shift_back(values, fraction):
    last = values.shape[-1] - 1
    column = lax.broadcasted_iota(jnp.int32, values.shape, values.ndim - 1)
    preceding = jnp.concatenate([jnp.zeros_like(values[..., :1]), values[..., :-1]], axis=-1)
    own_part = jnp.where(column < last, (1.0 - fraction) * values, values)
    return own_part + fraction * preceding


def smooth_rows(padded, taps, count):
    total = taps[0] * padded[..., 0:count, :]
    for offset in range(1, taps.shape[0]):
        total = total + taps[offset] * padded[..., offset:offset + count, :]
    return total


def smooth_cols(padded, taps, count):
    total = taps[0] * padded[..., 0:count]
    for offset in range(1, taps.shape[0]):
        total = total + taps[offset] * padded[..., offset:offset + count]
    return total


def blur_field(field, taps_rows, taps_cols):
    half = taps_rows.shape[0] // 2
    padded = jnp.pad(field, ((0, 0), (half, half), (0, 0)))
    rows_done = smooth_rows(padded, taps_rows, field.shape[1])
    padded = jnp.pad(rows_done, ((0, 0), (0, 0), (half, half)))
    return smooth_cols(padded, taps_cols, field.shape[2])


def reference(estimate, views, psf_rows, psf_cols, shifts, codes):
    groups = codes.shape[2]
    depth, total_rows, total_cols = estimate.shape
    tile_cols = total_cols // groups
    block_count = total_rows // BR
    kern_rows = psf_rows / jnp.sum(psf_rows, axis=1, keepdims=True)
    kern_cols = psf_cols / jnp.sum(psf_cols, axis=1, keepdims=True)
    peer_ids = jnp.arange(groups, dtype=jnp.int32)
    for sweep in range(ITERS):
        blocked = estimate.reshape(depth, block_count, BR, groups, tile_cols)
        summed = jnp.zeros(estimate.shape, jnp.float32)
        for view_id in range(V):
            fraction = (codes[view_id].astype(jnp.float32) / 16.0)[None, :, None, :, None]
            fetch = ((peer_ids[None, :] + shifts[view_id][:, None]) % groups).astype(jnp.int32)
            fetch_index = jnp.broadcast_to(fetch[None, :, None, :, None], blocked.shape)
            moved = jnp.take_along_axis(blocked, fetch_index, axis=3)
            view_est = shift_in(moved, fraction).reshape(depth, total_rows, total_cols)
            blurred = blur_field(view_est, kern_rows[view_id], kern_cols[view_id])
            ratio = views[view_id].astype(jnp.float32) / blurred
            back = blur_field(ratio, kern_rows[view_id][::-1], kern_cols[view_id][::-1])
            returned = shift_back(back.reshape(blocked.shape), fraction)
            home = ((peer_ids[None, :] - shifts[view_id][:, None]) % groups).astype(jnp.int32)
            home_index = jnp.broadcast_to(home[None, :, None, :, None], blocked.shape)
            summed = summed + jnp.take_along_axis(returned, home_index, axis=3).reshape(estimate.shape)
        estimate = estimate * (summed / V)
    return estimate
```

```python
import functools

import jax
import jax.numpy as jnp
from jax import lax
from jax.experimental import pallas as pl
from jax.experimental.pallas import tpu as pltpu
from jax.sharding import PartitionSpec as P

ITERS = 2
MESH = pl.DeviceIdType.MESH
F32 = jnp.float32
BF16 = jnp.bfloat16
HALO = 4
NEAR = 2


def with_halo(block, sides, width):
    for axis, dim in sides:
        count = lax.axis_size(axis)
        forward = [(i, i + 1) for i in range(count - 1)]
        backward = [(target, source) for source, target in forward]
        low = lax.ppermute(
            lax.slice_in_dim(block, block.shape[dim] - width, None, axis=dim), axis, forward
        )
        high = lax.ppermute(lax.slice_in_dim(block, 0, width, axis=dim), axis, backward)
        block = jnp.concatenate([low, block, high], axis=dim)
    return block


def shift_in(values, fraction):
    last = values.shape[-1] - 1
    column = lax.broadcasted_iota(jnp.int32, values.shape, values.ndim - 1)
    following = jnp.concatenate([values[..., 1:], values[..., -1:]], axis=-1)
    return jnp.where(column < last, (1.0 - fraction) * values + fraction * following, values)


def shift_back(values, fraction):
    last = values.shape[-1] - 1
    column = lax.broadcasted_iota(jnp.int32, values.shape, values.ndim - 1)
    preceding = jnp.concatenate([jnp.zeros_like(values[..., :1]), values[..., :-1]], axis=-1)
    own_part = jnp.where(column < last, (1.0 - fraction) * values, values)
    return own_part + fraction * preceding


def smooth_rows(padded, taps, count):
    total = taps[0] * padded[..., 0:count, :]
    for offset in range(1, taps.shape[0]):
        total = total + taps[offset] * padded[..., offset : offset + count, :]
    return total


def smooth_cols(padded, taps, count):
    total = taps[0] * padded[..., 0:count]
    for offset in range(1, taps.shape[0]):
        total = total + taps[offset] * padded[..., offset : offset + count]
    return total


def tile_body(estimate, views, psf_rows, psf_cols, shifts, codes):
    highest = lax.Precision.HIGHEST
    groups = lax.axis_size("gy")
    column = lax.axis_index("gy")
    views_n, depth, tile_rows, tile_cols = views.shape
    blocks_n = shifts.shape[1]
    block_rows = tile_rows // blocks_n
    capacity = 1 + (blocks_n + groups - 2) // groups
    tap_count = psf_rows.shape[1]
    half = tap_count // 2
    kern_rows = psf_rows / jnp.sum(psf_rows, axis=1, keepdims=True)
    kern_cols = psf_cols / jnp.sum(psf_cols, axis=1, keepdims=True)
    taps_rows = kern_rows.T.reshape(tap_count, views_n, 1, 1, 1)
    taps_cols = kern_cols.T.reshape(tap_count, views_n, 1, 1, 1)
    flipped_rows = kern_rows[:, ::-1].T.reshape(tap_count, views_n, 1, 1, 1)
    flipped_cols = kern_cols[:, ::-1].T.reshape(tap_count, views_n, 1, 1, 1)
    fraction = (codes[:, :, 0].astype(jnp.float32) / 16.0)[:, None, :, None, None]
    block_ids = jnp.arange(blocks_n, dtype=jnp.int32)
    same_shift = shifts[:, :, None] == shifts[:, None, :]
    earlier = block_ids[None, None, :] < block_ids[None, :, None]
    slot_rank = jnp.sum((same_shift & earlier).astype(jnp.int32), axis=2)
    peer_ids = jnp.arange(groups, dtype=jnp.int32)
    slot_ids = jnp.arange(capacity, dtype=jnp.int32)
    source_peer = (column + shifts) % groups
    target_peer = (column - shifts) % groups
    send_hot = (
        (peer_ids[None, :, None, None] == target_peer[:, None, None, :])
        & (slot_ids[None, None, :, None] == slot_rank[:, None, None, :])
    ).astype(jnp.float32)
    recv_hot = (
        (peer_ids[None, None, :, None] == source_peer[:, :, None, None])
        & (slot_ids[None, None, None, :] == slot_rank[:, :, None, None])
    ).astype(jnp.float32)
    for sweep in range(ITERS):
        blocked = estimate.reshape(depth, blocks_n, block_rows, tile_cols)
        outgoing = jnp.einsum("vpqk,zkrw->pvqzrw", send_hot, blocked, precision=highest)
        arriving = lax.all_to_all(outgoing, "gy", split_axis=0, concat_axis=0, tiled=True)
        view_blocks = jnp.einsum("vkpq,pvqzrw->vzkrw", recv_hot, arriving, precision=highest)
        view_est = shift_in(view_blocks, fraction).reshape(views_n, depth, tile_rows, tile_cols)
        padded = with_halo(view_est, (("gx", 2), ("gy", 3)), half)
        rows_done = smooth_rows(padded, taps_rows, tile_rows)
        blurred = smooth_cols(rows_done, taps_cols, tile_cols)
        ratio = views.astype(jnp.float32) / blurred
        padded_ratio = with_halo(ratio, (("gx", 2), ("gy", 3)), half)
        rows_back = smooth_rows(padded_ratio, flipped_rows, tile_rows)
        back = smooth_cols(rows_back, flipped_cols, tile_cols)
        returned = shift_back(
            back.reshape(views_n, depth, blocks_n, block_rows, tile_cols), fraction
        )
        leaving = jnp.einsum("vkpq,vzkrw->pvqzrw", recv_hot, returned, precision=highest)
        coming = lax.all_to_all(leaving, "gy", split_axis=0, concat_axis=0, tiled=True)
        summed = jnp.einsum("vpqk,pvqzrw->zkrw", send_hot, coming, precision=highest)
        estimate = estimate * (summed.reshape(depth, tile_rows, tile_cols) / views_n)
    return estimate


def split_store(ref, index, value):
    high = value.astype(BF16)
    ref[(0,) + index] = high
    ref[(1,) + index] = (value - high.astype(F32)).astype(BF16)


def product(left, right, dims):
    return lax.dot_general(left, right, (dims, ((), ())), preferred_element_type=F32)


def split(value):
    high = value.astype(BF16)
    return high, (value - high.astype(F32)).astype(BF16)


def rows_by(band, field):
    high, low = split(field)
    dims = ((1,), (0,))
    return (
        product(band[0], high, dims) + product(band[0], low, dims) + product(band[1], high, dims)
    )


def cols_by(field, band, side):
    high, low = split(field)
    dims = ((1,), (side,))
    return (
        product(high, band[0], dims) + product(low, band[0], dims) + product(high, band[1], dims)
    )


def taps_of(ref, view):
    taps = [ref[view, t] for t in range(ref.shape[1])]
    return taps, functools.reduce(lambda a, b: a + b, taps)


def banded(taps, total, offset):
    value = jnp.zeros(offset.shape, F32)
    for t, tap in enumerate(taps):
        value = jnp.where(offset == t, tap, value)
    return value / jnp.full(offset.shape, total, F32)


def kernel(
    gx_n, gy_n, est_ref, views_ref, meta_ref, psf_rows_ref, psf_cols_ref, out_ref,
    est_band, views_out, views_band, meta_band, frac_full, shift_full, sums_out, sums_in,
    band_fwd, band_back, band_cols,
    gather_s, gather_r, halo_s, halo_r, sums_s, sums_r, views_s, views_r, near_s, near_r,
    meta_s, meta_r, edge_s, edge_r,
):
    depth, blocks_n, block_rows, width = est_ref.shape
    tile_rows = blocks_n * block_rows
    band_rows = (blocks_n + 2 * HALO) * block_rows
    near_rows = (blocks_n + 2 * NEAR) * block_rows
    band_cells = gy_n * width
    half = psf_rows_ref.shape[1] // 2
    g = lax.axis_index("gx")
    c = lax.axis_index("gy")
    peers = [lax.rem(c + k, gy_n) for k in range(1, gy_n)]
    above = lax.rem(g + gx_n - 1, gx_n)
    below = lax.rem(g + 1, gx_n)
    pending = []

    def send(src, dst, send_sem, recv_sem, target):
        copy = pltpu.make_async_remote_copy(
            src_ref=src, dst_ref=dst, send_sem=send_sem, recv_sem=recv_sem,
            device_id=target, device_id_type=MESH,
        )
        copy.start()
        pending.append(copy)
        return copy

    barrier = pltpu.get_barrier_semaphore()
    for target in [{"gy": p} for p in peers] + [{"gx": above}, {"gx": below}]:
        pl.semaphore_signal(barrier, inc=1, device_id=target, device_id_type=MESH)
    own = pl.ds(HALO, blocks_n)
    for plane in range(depth):
        est_band[0, plane, c, own] = est_ref[plane]
    meta_band[c, :, pl.ds(8, blocks_n)] = meta_ref[c]
    for plane in range(depth):
        for view in range(gy_n):
            views_out[view, plane] = (
                views_ref[view, plane].astype(F32).reshape(blocks_n, block_rows, width)
            )
        views_band[plane, c, pl.ds(NEAR, blocks_n)] = views_out[c, plane]
    pl.semaphore_wait(barrier, gy_n + 1)

    def send_estimate(sweep, plane):
        place = est_band.at[sweep, plane, c, own]
        return [
            send(place, place, gather_s.at[sweep, plane, k], gather_r.at[sweep, plane, k], {"gy": p})
            for k, p in enumerate(peers)
        ]

    def send_views(plane):
        return [
            send(
                views_out.at[p, plane], views_band.at[plane, c, pl.ds(NEAR, blocks_n)],
                views_s.at[plane, k], views_r.at[plane, k], {"gy": p},
            )
            for k, p in enumerate(peers)
        ]

    meta_copies = [
        send(
            meta_ref.at[p], meta_band.at[c, :, pl.ds(8, blocks_n)],
            meta_s.at[k], meta_r.at[k], {"gy": p},
        )
        for k, p in enumerate(peers)
    ]
    gathers = {}
    view_copies = {}
    for plane in range(depth):
        gathers[0, plane] = send_estimate(0, plane)
        view_copies[plane] = send_views(plane)

    taps, total = taps_of(psf_rows_ref, c)
    first_row = jnp.where(g == 0, 0, -HALO * block_rows)
    last_row = jnp.where(g == gx_n - 1, tile_rows, tile_rows + HALO * block_rows)
    row = lax.broadcasted_iota(jnp.int32, (near_rows, band_rows), 0) - NEAR * block_rows
    col = lax.broadcasted_iota(jnp.int32, (near_rows, band_rows), 1) - HALO * block_rows
    inside = (col >= first_row) & (col < last_row)
    outer = (row < first_row) | (row >= last_row)
    value = banded(taps, total, col - row + half)
    split_store(band_fwd, (), jnp.where(inside | outer, value, 0.0))
    row = lax.broadcasted_iota(jnp.int32, (tile_rows, near_rows), 0)
    col = lax.broadcasted_iota(jnp.int32, (tile_rows, near_rows), 1) - NEAR * block_rows
    inside = (col >= first_row) & (col < last_row)
    value = banded(taps, total, row - col + half)
    split_store(band_back, (), jnp.where(inside, value, 0.0))
    taps, total = taps_of(psf_cols_ref, c)
    row = lax.broadcasted_iota(jnp.int32, (width, width), 0)
    col = lax.broadcasted_iota(jnp.int32, (width, width), 1)
    band_cols[...] = jnp.zeros(band_cols.shape, BF16)
    for step in (-1, 0, 1):
        value = banded(taps, total, row - col + step * width + half)
        for j in range(gy_n):
            if 0 <= j + step < gy_n:
                split_store(
                    band_cols, (pl.ds((j + step) * width, width), pl.ds(j * width, width)), value
                )

    for copy in meta_copies:
        copy.wait_recv()
    edges = [
        send(
            meta_band.at[:, :, pl.ds(8, 8)], meta_band.at[:, :, pl.ds(8 + blocks_n, 8)],
            edge_s.at[0], edge_r.at[0], {"gx": above},
        ),
        send(
            meta_band.at[:, :, pl.ds(blocks_n, 8)], meta_band.at[:, :, pl.ds(0, 8)],
            edge_s.at[1], edge_r.at[1], {"gx": below},
        ),
    ]
    for copy in edges:
        copy.wait_recv()

    def spread(b, carry):
        for j in range(gy_n):
            line = meta_band[j, 0, pl.ds(b + 8 - HALO, 1), :]
            frac_full[j, b] = jnp.broadcast_to(line, (block_rows, width))
        line = meta_band[0, 1, pl.ds(b + 8 - HALO, 1), :]
        shift_full[b] = jnp.broadcast_to(line, (block_rows, width))
        return carry

    lax.fori_loop(0, blocks_n + 2 * HALO, spread, 0)

    def pick(shift, tiles, first, sign):
        value = tiles[first % gy_n]
        for k in range(1, gy_n):
            value = jnp.where(shift == float(k), tiles[(first + sign * k) % gy_n], value)
        return value

    def correction(sweep, plane):
        for copy in gathers[sweep, plane]:
            copy.wait_recv()
        band = est_band.at[sweep, plane]
        halos = [
            send(
                band.at[:, pl.ds(HALO, HALO)], band.at[:, pl.ds(HALO + blocks_n, HALO)],
                halo_s.at[sweep, plane, 0], halo_r.at[sweep, plane, 0], {"gx": above},
            ),
            send(
                band.at[:, pl.ds(blocks_n, HALO)], band.at[:, pl.ds(0, HALO)],
                halo_s.at[sweep, plane, 1], halo_r.at[sweep, plane, 1], {"gx": below},
            ),
        ]
        for copy in halos:
            copy.wait_recv()
        shift = shift_full[...]
        lane = lax.broadcasted_iota(jnp.int32, (band_rows, width), 1)
        tiles = [band[j] for j in range(gy_n)]
        parts = []
        for j in range(gy_n):
            moved = pick(shift, tiles, j, 1).reshape(band_rows, width)
            fraction = jnp.where(lane < width - 1, frac_full[j].reshape(band_rows, width), 0.0)
            following = pltpu.roll(moved, width - 1, 1)
            parts.append((1.0 - fraction) * moved + fraction * following)
        view_est = jnp.concatenate(parts, axis=1)
        blurred = cols_by(rows_by(band_fwd, view_est), band_cols, 0)
        if sweep == 0:
            for copy in view_copies[plane]:
                copy.wait_recv()
            seen = views_band.at[plane]
            nears = [
                send(
                    seen.at[:, pl.ds(NEAR, NEAR)], seen.at[:, pl.ds(NEAR + blocks_n, NEAR)],
                    near_s.at[plane, 0], near_r.at[plane, 0], {"gx": above},
                ),
                send(
                    seen.at[:, pl.ds(blocks_n, NEAR)], seen.at[:, pl.ds(0, NEAR)],
                    near_s.at[plane, 1], near_r.at[plane, 1], {"gx": below},
                ),
            ]
            for copy in nears:
                copy.wait_recv()
        seen = jnp.concatenate(
            [views_band[plane, j].reshape(near_rows, width) for j in range(gy_n)], axis=1
        )
        ratio = seen / blurred
        back = cols_by(rows_by(band_back, ratio), band_cols, 1)
        lane = lax.broadcasted_iota(jnp.int32, (tile_rows, width), 1)
        returned = []
        for j in range(gy_n):
            tile = back[:, j * width : (j + 1) * width]
            fraction = frac_full[j, own].reshape(tile_rows, width)
            kept = jnp.where(lane < width - 1, 1.0 - fraction, 1.0)
            passed = jnp.where(lane > 0, fraction, 0.0)
            value = kept * tile + passed * pltpu.roll(tile, 1, 1)
            returned.append(value.reshape(blocks_n, block_rows, width))
        shift = shift_full[own]
        for j in range(gy_n):
            sums_out[sweep, plane, j] = pick(shift, returned, j, -1)
        return [
            send(
                sums_out.at[sweep, plane, p], sums_in.at[sweep, plane, c],
                sums_s.at[sweep, plane, k], sums_r.at[sweep, plane, k], {"gy": p},
            )
            for k, p in enumerate(peers)
        ]

    for sweep in range(ITERS):
        sums = [correction(sweep, plane) for plane in range(depth)]
        for plane in range(depth):
            summed = sums_out[sweep, plane, c]
            for copy in sums[plane]:
                copy.wait_recv()
            for p in peers:
                summed = summed + sums_in[sweep, plane, p]
            updated = est_band[sweep, plane, c, own] * (summed / views_ref.shape[0])
            if sweep + 1 < ITERS:
                est_band[sweep + 1, plane, c, own] = updated
                gathers[sweep + 1, plane] = send_estimate(sweep + 1, plane)
            else:
                out_ref[plane] = updated
    for copy in pending:
        copy.wait_send()


def band_body(gx_n, gy_n, estimate, views, psf_rows, psf_cols, shifts, codes):
    views_n, depth, tile_rows, width = views.shape
    blocks_n = shifts.shape[1]
    block_rows = tile_rows // blocks_n
    fraction = codes[:, :, 0].astype(F32) / 16.0
    meta = jnp.stack([fraction, shifts.astype(F32)], axis=1)
    meta = jnp.broadcast_to(meta[..., None], (views_n, 2, blocks_n, width))
    near_rows = tile_rows + 2 * NEAR * block_rows
    band_rows = tile_rows + 2 * HALO * block_rows
    others = gy_n - 1
    vmem = pltpu.VMEM
    dma = pltpu.SemaphoreType.DMA
    out = pl.pallas_call(
        functools.partial(kernel, gx_n, gy_n),
        out_shape=jax.ShapeDtypeStruct((depth, blocks_n, block_rows, width), F32),
        in_specs=[pl.BlockSpec(memory_space=pltpu.VMEM)] * 3
        + [pl.BlockSpec(memory_space=pltpu.SMEM)] * 2,
        out_specs=pl.BlockSpec(memory_space=pltpu.VMEM),
        scratch_shapes=[
            vmem((ITERS, depth, gy_n, blocks_n + 2 * HALO, block_rows, width), F32),
            vmem((gy_n, depth, blocks_n, block_rows, width), F32),
            vmem((depth, gy_n, blocks_n + 2 * NEAR, block_rows, width), F32),
            vmem((gy_n, 2, blocks_n + 16, width), F32),
            vmem((gy_n, blocks_n + 2 * HALO, block_rows, width), F32),
            vmem((blocks_n + 2 * HALO, block_rows, width), F32),
            vmem((ITERS, depth, gy_n, blocks_n, block_rows, width), F32),
            vmem((ITERS, depth, gy_n, blocks_n, block_rows, width), F32),
            vmem((2, near_rows, band_rows), BF16),
            vmem((2, tile_rows, near_rows), BF16),
            vmem((2, gy_n * width, gy_n * width), BF16),
            dma((ITERS, depth, others)), dma((ITERS, depth, others)),
            dma((ITERS, depth, 2)), dma((ITERS, depth, 2)),
            dma((ITERS, depth, others)), dma((ITERS, depth, others)),
            dma((depth, others)), dma((depth, others)),
            dma((depth, 2)), dma((depth, 2)),
            dma((others,)), dma((others,)),
            dma((2,)), dma((2,)),
        ],
        compiler_params=pltpu.CompilerParams(
            collective_id=0, has_side_effects=True, vmem_limit_bytes=48 * 1024 * 1024
        ),
    )(estimate.reshape(depth, blocks_n, block_rows, width), views, meta, psf_rows, psf_cols)
    return out.reshape(depth, tile_rows, width)


def solution(mesh):
    placed = (
        P(None, "gx", "gy"),
        P(None, None, "gx", "gy"),
        P(),
        P(),
        P(None, "gx"),
        P(None, "gx", "gy"),
    )
    gx_n, gy_n = mesh.shape["gx"], mesh.shape["gy"]

    def body(estimate, views, *rest):
        if gy_n == views.shape[0] and gx_n > 1:
            return band_body(gx_n, gy_n, estimate, views, *rest)
        return tile_body(estimate, views, *rest)

    return jax.shard_map(
        body, mesh=mesh, in_specs=placed, out_specs=P(None, "gx", "gy"), check_vma=False
    )
```

```python
import functools

import jax
import jax.numpy as jnp
from jax import lax
from jax.experimental import pallas as pl
from jax.experimental.pallas import tpu as pltpu
from jax.sharding import PartitionSpec as P

ITERS = 2
MESH = pl.DeviceIdType.MESH
F32 = jnp.float32
BF16 = jnp.bfloat16
HALO = 4
NEAR = 2


def with_halo(block, sides, width):
    for axis, dim in sides:
        count = lax.axis_size(axis)
        forward = [(i, i + 1) for i in range(count - 1)]
        backward = [(target, source) for source, target in forward]
        low = lax.ppermute(
            lax.slice_in_dim(block, block.shape[dim] - width, None, axis=dim), axis, forward
        )
        high = lax.ppermute(lax.slice_in_dim(block, 0, width, axis=dim), axis, backward)
        block = jnp.concatenate([low, block, high], axis=dim)
    return block


def shift_in(values, fraction):
    last = values.shape[-1] - 1
    column = lax.broadcasted_iota(jnp.int32, values.shape, values.ndim - 1)
    following = jnp.concatenate([values[..., 1:], values[..., -1:]], axis=-1)
    return jnp.where(column < last, (1.0 - fraction) * values + fraction * following, values)


def shift_back(values, fraction):
    last = values.shape[-1] - 1
    column = lax.broadcasted_iota(jnp.int32, values.shape, values.ndim - 1)
    preceding = jnp.concatenate([jnp.zeros_like(values[..., :1]), values[..., :-1]], axis=-1)
    own_part = jnp.where(column < last, (1.0 - fraction) * values, values)
    return own_part + fraction * preceding


def smooth_rows(padded, taps, count):
    total = taps[0] * padded[..., 0:count, :]
    for offset in range(1, taps.shape[0]):
        total = total + taps[offset] * padded[..., offset : offset + count, :]
    return total


def smooth_cols(padded, taps, count):
    total = taps[0] * padded[..., 0:count]
    for offset in range(1, taps.shape[0]):
        total = total + taps[offset] * padded[..., offset : offset + count]
    return total


def tile_body(estimate, views, psf_rows, psf_cols, shifts, codes):
    highest = lax.Precision.HIGHEST
    groups = lax.axis_size("gy")
    column = lax.axis_index("gy")
    views_n, depth, tile_rows, tile_cols = views.shape
    blocks_n = shifts.shape[1]
    block_rows = tile_rows // blocks_n
    capacity = 1 + (blocks_n + groups - 2) // groups
    tap_count = psf_rows.shape[1]
    half = tap_count // 2
    kern_rows = psf_rows / jnp.sum(psf_rows, axis=1, keepdims=True)
    kern_cols = psf_cols / jnp.sum(psf_cols, axis=1, keepdims=True)
    taps_rows = kern_rows.T.reshape(tap_count, views_n, 1, 1, 1)
    taps_cols = kern_cols.T.reshape(tap_count, views_n, 1, 1, 1)
    flipped_rows = kern_rows[:, ::-1].T.reshape(tap_count, views_n, 1, 1, 1)
    flipped_cols = kern_cols[:, ::-1].T.reshape(tap_count, views_n, 1, 1, 1)
    fraction = (codes[:, :, 0].astype(jnp.float32) / 16.0)[:, None, :, None, None]
    block_ids = jnp.arange(blocks_n, dtype=jnp.int32)
    same_shift = shifts[:, :, None] == shifts[:, None, :]
    earlier = block_ids[None, None, :] < block_ids[None, :, None]
    slot_rank = jnp.sum((same_shift & earlier).astype(jnp.int32), axis=2)
    peer_ids = jnp.arange(groups, dtype=jnp.int32)
    slot_ids = jnp.arange(capacity, dtype=jnp.int32)
    source_peer = (column + shifts) % groups
    target_peer = (column - shifts) % groups
    send_hot = (
        (peer_ids[None, :, None, None] == target_peer[:, None, None, :])
        & (slot_ids[None, None, :, None] == slot_rank[:, None, None, :])
    ).astype(jnp.float32)
    recv_hot = (
        (peer_ids[None, None, :, None] == source_peer[:, :, None, None])
        & (slot_ids[None, None, None, :] == slot_rank[:, :, None, None])
    ).astype(jnp.float32)
    for sweep in range(ITERS):
        blocked = estimate.reshape(depth, blocks_n, block_rows, tile_cols)
        outgoing = jnp.einsum("vpqk,zkrw->pvqzrw", send_hot, blocked, precision=highest)
        arriving = lax.all_to_all(outgoing, "gy", split_axis=0, concat_axis=0, tiled=True)
        view_blocks = jnp.einsum("vkpq,pvqzrw->vzkrw", recv_hot, arriving, precision=highest)
        view_est = shift_in(view_blocks, fraction).reshape(views_n, depth, tile_rows, tile_cols)
        padded = with_halo(view_est, (("gx", 2), ("gy", 3)), half)
        rows_done = smooth_rows(padded, taps_rows, tile_rows)
        blurred = smooth_cols(rows_done, taps_cols, tile_cols)
        ratio = views.astype(jnp.float32) / blurred
        padded_ratio = with_halo(ratio, (("gx", 2), ("gy", 3)), half)
        rows_back = smooth_rows(padded_ratio, flipped_rows, tile_rows)
        back = smooth_cols(rows_back, flipped_cols, tile_cols)
        returned = shift_back(
            back.reshape(views_n, depth, blocks_n, block_rows, tile_cols), fraction
        )
        leaving = jnp.einsum("vkpq,vzkrw->pvqzrw", recv_hot, returned, precision=highest)
        coming = lax.all_to_all(leaving, "gy", split_axis=0, concat_axis=0, tiled=True)
        summed = jnp.einsum("vpqk,pvqzrw->zkrw", send_hot, coming, precision=highest)
        estimate = estimate * (summed.reshape(depth, tile_rows, tile_cols) / views_n)
    return estimate


def split_store(ref, index, value):
    high = value.astype(BF16)
    ref[(0,) + index] = high
    ref[(1,) + index] = (value - high.astype(F32)).astype(BF16)


def product(left, right, dims):
    return lax.dot_general(left, right, (dims, ((), ())), preferred_element_type=F32)


def split(value):
    high = value.astype(BF16)
    return high, (value - high.astype(F32)).astype(BF16)


def rows_by(band, field):
    high, low = split(field)
    dims = ((1,), (0,))
    return (
        product(band[0], high, dims) + product(band[0], low, dims) + product(band[1], high, dims)
    )


def cols_by(field, band, side):
    width = band.shape[-1] // 2
    rows = field.shape[0]
    count = field.shape[1] // width - 1
    high, low = split(field)
    windows = [part[:, j * width : (j + 2) * width] for part in (high, low) for j in range(count)]
    dims = ((1,), (side,))
    first = product(jnp.concatenate(windows, axis=0), band[0], dims)
    second = product(jnp.concatenate(windows[:count], axis=0), band[1], dims)
    done = first[: count * rows] + first[count * rows :] + second
    done = [done[j * rows : (j + 1) * rows] for j in range(count)]
    lane = lax.broadcasted_iota(jnp.int32, (rows, width), 1)
    tiles = [done[0][:, :width]]
    for j in range(count - 1):
        tiles.append(jnp.where(lane < width // 2, done[j][:, width:], done[j + 1][:, :width]))
    tiles.append(done[-1][:, width:])
    return tiles


def taps_of(ref, view):
    taps = [ref[view, t] for t in range(ref.shape[1])]
    return taps, functools.reduce(lambda a, b: a + b, taps)


def banded(taps, total, offset):
    value = jnp.zeros(offset.shape, F32)
    for t, tap in enumerate(taps):
        value = jnp.where(offset == t, tap, value)
    return value / jnp.full(offset.shape, total, F32)


def kernel(
    gx_n, gy_n, est_ref, views_ref, meta_ref, psf_rows_ref, psf_cols_ref, out_ref,
    est_band, views_out, views_band, meta_band, lines, frac_full, shift_full, out_own, out_in,
    band_fwd, band_back, band_cols,
    gather_s, gather_r, halo_s, halo_r, views_s, views_r, near_s, near_r,
    meta_s, meta_r, edge_s, edge_r, out_s, out_r,
):
    views_n, depth, _, width = views_ref.shape
    blocks_n, block_rows = est_ref.shape[1:3]
    part_n = blocks_n // 2
    part_rows = part_n * block_rows
    band_rows = (part_n + 2 * HALO) * block_rows
    near_rows = (part_n + 2 * NEAR) * block_rows
    half = psf_rows_ref.shape[1] // 2
    g = lax.axis_index("gx")
    c = lax.axis_index("gy")

    def place_of(device):
        return device // 2, lax.rem(device + g, 2)

    plane, h = place_of(c)
    peers = [lax.rem(c + k, gy_n) for k in range(1, gy_n)]
    partner = {"gy": c + 1 - 2 * lax.rem(c, 2)}
    beside = {"gx": lax.rem(g - 1 + 2 * h + gx_n, gx_n)}
    pending = []

    def send(src, dst, send_sem, recv_sem, target):
        copy = pltpu.make_async_remote_copy(
            src_ref=src, dst_ref=dst, send_sem=send_sem, recv_sem=recv_sem,
            device_id=target, device_id_type=MESH,
        )
        copy.start()
        pending.append(copy)
        return copy

    barrier = pltpu.get_barrier_semaphore()
    for target in [{"gy": p} for p in peers] + [beside]:
        pl.semaphore_signal(barrier, inc=1, device_id=target, device_id_type=MESH)
    for view in range(views_n):
        for layer in range(depth):
            views_out[view, layer] = (
                views_ref[view, layer].astype(F32).reshape(blocks_n, block_rows, width)
            )
    pl.semaphore_wait(barrier, gy_n)

    meta_copies = [
        send(meta_ref, meta_band.at[c, pl.ds(1, 2)], meta_s.at[k], meta_r.at[k], {"gy": p})
        for k, p in enumerate(peers)
    ]
    est_n = part_n + HALO
    view_n = part_n + NEAR
    gathers = []
    for k, p in enumerate(peers):
        layer, other = place_of(p)
        gathers.append(
            send(
                est_ref.at[layer, pl.ds(HALO * other, est_n)],
                est_band.at[0, c, pl.ds(HALO - HALO * other, est_n)],
                gather_s.at[k], gather_r.at[k], {"gy": p},
            )
        )
    view_copies = []
    for view in range(views_n):
        copies = []
        for k, p in enumerate(peers):
            layer, other = place_of(p)
            copies.append(
                send(
                    views_out.at[view, layer, pl.ds((part_n - NEAR) * other, view_n)],
                    views_band.at[view, c, pl.ds(NEAR - NEAR * other, view_n)],
                    views_s.at[view, k], views_r.at[view, k], {"gy": p},
                )
            )
        view_copies.append(copies)
    meta_band[c, pl.ds(1, 2)] = meta_ref[...]
    est_band[0, c, pl.ds(HALO - HALO * h, est_n)] = est_ref[plane, pl.ds(HALO * h, est_n)]
    for view in range(views_n):
        views_band[view, c, pl.ds(NEAR - NEAR * h, view_n)] = views_out[
            view, plane, pl.ds((part_n - NEAR) * h, view_n)
        ]

    for copy in meta_copies:
        copy.wait_recv()
    edge = send(
        meta_band.at[:, 1 + h], meta_band.at[:, 3 - 3 * h], edge_s.at[0], edge_r.at[0], beside
    )
    for copy in gathers:
        copy.wait_recv()
    halo = send(
        est_band.at[0, :, pl.ds(HALO + (part_n - HALO) * h, HALO)],
        est_band.at[0, :, pl.ds((part_n + HALO) * (1 - h), HALO)],
        halo_s.at[0], halo_r.at[0], beside,
    )

    first_row = jnp.where((g == 0) & (h == 0), 0, -HALO * block_rows)
    last_row = jnp.where((g == gx_n - 1) & (h == 1), part_rows, part_rows + HALO * block_rows)
    for view in range(views_n):
        taps, total = taps_of(psf_rows_ref, view)
        row = lax.broadcasted_iota(jnp.int32, (near_rows, band_rows), 0) - NEAR * block_rows
        col = lax.broadcasted_iota(jnp.int32, (near_rows, band_rows), 1) - HALO * block_rows
        inside = (col >= first_row) & (col < last_row)
        outer = (row < first_row) | (row >= last_row)
        value = banded(taps, total, col - row + half)
        split_store(band_fwd.at[view], (), jnp.where(inside | outer, value, 0.0))
        row = lax.broadcasted_iota(jnp.int32, (part_rows, near_rows), 0)
        col = lax.broadcasted_iota(jnp.int32, (part_rows, near_rows), 1) - NEAR * block_rows
        inside = (col >= first_row) & (col < last_row)
        value = banded(taps, total, row - col + half)
        split_store(band_back.at[view], (), jnp.where(inside, value, 0.0))
        taps, total = taps_of(psf_cols_ref, view)
        row = lax.broadcasted_iota(jnp.int32, (width, width), 0)
        col = lax.broadcasted_iota(jnp.int32, (width, width), 1)
        value = banded(taps, total, row - col + half)
        low, high = pl.ds(0, width), pl.ds(width, width)
        split_store(band_cols.at[view], (low, low), value)
        split_store(band_cols.at[view], (high, high), value)
        row, col = row[:16], col[:16]
        blank = jnp.zeros((width - 16, width), F32)
        value = banded(taps, total, row + width - col + half)
        split_store(band_cols.at[view], (high, low), jnp.concatenate([value, blank], axis=0))
        value = banded(taps, total, row - 16 - col + half)
        split_store(band_cols.at[view], (low, high), jnp.concatenate([blank, value], axis=0))

    edge.wait_recv()
    for j in range(gy_n):
        found = meta_band[j].reshape(4 * 8, width)
        for view in range(views_n):
            lines[view, j] = jnp.broadcast_to(found[:, view : view + 1], found.shape)
            if j == 0:
                near = found[:, views_n + view : views_n + view + 1]
                lines[view, gy_n] = jnp.broadcast_to(near, found.shape)

    def spread(b, carry):
        place = pl.ds(b + 8 - HALO + part_n * h, 1)
        for view in range(views_n):
            for j in range(gy_n):
                frac_full[view, j, b] = jnp.broadcast_to(
                    lines[view, j, place, :], (block_rows, width)
                )
            shift_full[view, b] = jnp.broadcast_to(
                lines[view, gy_n, place, :], (block_rows, width)
            )
        return carry

    lax.fori_loop(0, part_n + 2 * HALO, spread, 0)
    halo.wait_recv()

    def pick(shift, tiles, first, sign):
        value = tiles[first % gy_n]
        for k in range(1, gy_n):
            value = jnp.where(shift == float(k), tiles[(first + sign * k) % gy_n], value)
        return value

    own = pl.ds(HALO, part_n)
    for sweep in range(ITERS):
        sums = None
        for view in range(views_n):
            if sweep == 0:
                for copy in view_copies[view]:
                    copy.wait_recv()
                near = send(
                    views_band.at[view, :, pl.ds(NEAR + (part_n - NEAR) * h, NEAR)],
                    views_band.at[view, :, pl.ds((part_n + NEAR) * (1 - h), NEAR)],
                    near_s.at[view], near_r.at[view], beside,
                )
            shift = shift_full[view]
            lane = lax.broadcasted_iota(jnp.int32, (band_rows, width), 1)
            tiles = [est_band[sweep, j] for j in range(gy_n)]
            parts = []
            for j in range(gy_n):
                moved = pick(shift, tiles, j, 1).reshape(band_rows, width)
                fraction = frac_full[view, j].reshape(band_rows, width)
                fraction = jnp.where(lane < width - 1, fraction, 0.0)
                following = pltpu.roll(moved, width - 1, 1)
                parts.append((1.0 - fraction) * moved + fraction * following)
            rows_done = rows_by(band_fwd.at[view], jnp.concatenate(parts, axis=1))
            blurred = cols_by(rows_done, band_cols.at[view], 0)
            if sweep == 0:
                near.wait_recv()
            ratio = [
                views_band[view, j].reshape(near_rows, width) / blurred[j] for j in range(gy_n)
            ]
            rows_back = rows_by(band_back.at[view], jnp.concatenate(ratio, axis=1))
            back = cols_by(rows_back, band_cols.at[view], 1)
            lane = lax.broadcasted_iota(jnp.int32, (part_rows, width), 1)
            returned = []
            for j in range(gy_n):
                fraction = frac_full[view, j, own].reshape(part_rows, width)
                kept = jnp.where(lane < width - 1, 1.0 - fraction, 1.0)
                passed = jnp.where(lane > 0, fraction, 0.0)
                value = kept * back[j] + passed * pltpu.roll(back[j], 1, 1)
                returned.append(value.reshape(part_n, block_rows, width))
            shift = shift_full[view, own]
            homes = [pick(shift, returned, j, -1) for j in range(gy_n)]
            sums = homes if sums is None else [a + b for a, b in zip(sums, homes)]
        updated = [est_band[sweep, j, own] * (sums[j] / views_n) for j in range(gy_n)]
        if sweep + 1 < ITERS:
            for j in range(gy_n):
                est_band[sweep + 1, j, own] = updated[j]
            band = est_band.at[sweep + 1]
            halos = [
                send(
                    band.at[:, pl.ds(part_n - (part_n - HALO) * h, HALO)],
                    band.at[:, pl.ds((part_n + HALO) * h, HALO)],
                    halo_s.at[2 * sweep + 1], halo_r.at[2 * sweep + 1], partner,
                ),
                send(
                    band.at[:, pl.ds(HALO + (part_n - HALO) * h, HALO)],
                    band.at[:, pl.ds((part_n + HALO) * (1 - h), HALO)],
                    halo_s.at[2 * sweep + 2], halo_r.at[2 * sweep + 2], beside,
                ),
            ]
            for copy in halos:
                copy.wait_recv()
    for j in range(gy_n):
        out_own[j] = updated[j]
    place = pl.ds(part_n * h, part_n)
    outs = [
        send(out_own.at[p], out_in.at[plane, place], out_s.at[k], out_r.at[k], {"gy": p})
        for k, p in enumerate(peers)
    ]
    out_in[plane, place] = out_own[c]
    for copy in outs:
        copy.wait_recv()
    out_ref[...] = out_in[...]
    for copy in pending:
        copy.wait_send()


def band_body(gx_n, gy_n, estimate, views, psf_rows, psf_cols, shifts, codes):
    views_n, depth, tile_rows, width = views.shape
    blocks_n = shifts.shape[1]
    block_rows = tile_rows // blocks_n
    fraction = codes[:, :, 0].astype(F32) / 16.0
    meta = jnp.concatenate([fraction, shifts.astype(F32)], axis=0).T
    meta = jnp.pad(meta, ((0, 0), (0, width - 2 * views_n))).reshape(2, 8, width)
    part_n = blocks_n // 2
    part_rows = part_n * block_rows
    near_rows = part_rows + 2 * NEAR * block_rows
    band_rows = part_rows + 2 * HALO * block_rows
    others = gy_n - 1
    vmem = pltpu.VMEM
    dma = pltpu.SemaphoreType.DMA
    out = pl.pallas_call(
        functools.partial(kernel, gx_n, gy_n),
        out_shape=jax.ShapeDtypeStruct((depth, blocks_n, block_rows, width), F32),
        in_specs=[pl.BlockSpec(memory_space=pltpu.VMEM)] * 3
        + [pl.BlockSpec(memory_space=pltpu.SMEM)] * 2,
        out_specs=pl.BlockSpec(memory_space=pltpu.VMEM),
        scratch_shapes=[
            vmem((ITERS, gy_n, part_n + 2 * HALO, block_rows, width), F32),
            vmem((views_n, depth, blocks_n, block_rows, width), F32),
            vmem((views_n, gy_n, part_n + 2 * NEAR, block_rows, width), F32),
            vmem((gy_n, 4, 8, width), F32),
            vmem((views_n, gy_n + 1, 4 * 8, width), F32),
            vmem((views_n, gy_n, part_n + 2 * HALO, block_rows, width), F32),
            vmem((views_n, part_n + 2 * HALO, block_rows, width), F32),
            vmem((gy_n, part_n, block_rows, width), F32),
            vmem((depth, blocks_n, block_rows, width), F32),
            vmem((views_n, 2, near_rows, band_rows), BF16),
            vmem((views_n, 2, part_rows, near_rows), BF16),
            vmem((views_n, 2, 2 * width, 2 * width), BF16),
            dma((others,)), dma((others,)),
            dma((2 * ITERS - 1,)), dma((2 * ITERS - 1,)),
            dma((views_n, others)), dma((views_n, others)),
            dma((views_n,)), dma((views_n,)),
            dma((others,)), dma((others,)),
            dma((1,)), dma((1,)),
            dma((others,)), dma((others,)),
        ],
        compiler_params=pltpu.CompilerParams(
            collective_id=0, has_side_effects=True, vmem_limit_bytes=48 * 1024 * 1024
        ),
    )(estimate.reshape(depth, blocks_n, block_rows, width), views, meta, psf_rows, psf_cols)
    return out.reshape(depth, tile_rows, width)


def solution(mesh):
    placed = (
        P(None, "gx", "gy"),
        P(None, None, "gx", "gy"),
        P(),
        P(),
        P(None, "gx"),
        P(None, "gx", "gy"),
    )
    gx_n, gy_n = mesh.shape["gx"], mesh.shape["gy"]

    def body(estimate, views, *rest):
        parts_n = 2 * estimate.shape[0]
        if gy_n == parts_n and gx_n % 2 == 0 and rest[2].shape[1] == 16:
            return band_body(gx_n, gy_n, estimate, views, *rest)
        return tile_body(estimate, views, *rest)

    return jax.shard_map(
        body, mesh=mesh, in_specs=placed, out_specs=P(None, "gx", "gy"), check_vma=False
    )
```

```python
import functools

import jax
import jax.numpy as jnp
from jax import lax
from jax.experimental import pallas as pl
from jax.experimental.pallas import tpu as pltpu
from jax.sharding import PartitionSpec as P

ITERS = 2
MESH = pl.DeviceIdType.MESH
F32 = jnp.float32
BF16 = jnp.bfloat16
HALO = 4
NEAR = 2


def with_halo(block, sides, width):
    for axis, dim in sides:
        count = lax.axis_size(axis)
        forward = [(i, i + 1) for i in range(count - 1)]
        backward = [(target, source) for source, target in forward]
        low = lax.ppermute(
            lax.slice_in_dim(block, block.shape[dim] - width, None, axis=dim), axis, forward
        )
        high = lax.ppermute(lax.slice_in_dim(block, 0, width, axis=dim), axis, backward)
        block = jnp.concatenate([low, block, high], axis=dim)
    return block


def shift_in(values, fraction):
    last = values.shape[-1] - 1
    column = lax.broadcasted_iota(jnp.int32, values.shape, values.ndim - 1)
    following = jnp.concatenate([values[..., 1:], values[..., -1:]], axis=-1)
    return jnp.where(column < last, (1.0 - fraction) * values + fraction * following, values)


def shift_back(values, fraction):
    last = values.shape[-1] - 1
    column = lax.broadcasted_iota(jnp.int32, values.shape, values.ndim - 1)
    preceding = jnp.concatenate([jnp.zeros_like(values[..., :1]), values[..., :-1]], axis=-1)
    own_part = jnp.where(column < last, (1.0 - fraction) * values, values)
    return own_part + fraction * preceding


def smooth_rows(padded, taps, count):
    total = taps[0] * padded[..., 0:count, :]
    for offset in range(1, taps.shape[0]):
        total = total + taps[offset] * padded[..., offset : offset + count, :]
    return total


def smooth_cols(padded, taps, count):
    total = taps[0] * padded[..., 0:count]
    for offset in range(1, taps.shape[0]):
        total = total + taps[offset] * padded[..., offset : offset + count]
    return total


def tile_body(estimate, views, psf_rows, psf_cols, shifts, codes):
    highest = lax.Precision.HIGHEST
    groups = lax.axis_size("gy")
    column = lax.axis_index("gy")
    views_n, depth, tile_rows, tile_cols = views.shape
    blocks_n = shifts.shape[1]
    block_rows = tile_rows // blocks_n
    capacity = 1 + (blocks_n + groups - 2) // groups
    tap_count = psf_rows.shape[1]
    half = tap_count // 2
    kern_rows = psf_rows / jnp.sum(psf_rows, axis=1, keepdims=True)
    kern_cols = psf_cols / jnp.sum(psf_cols, axis=1, keepdims=True)
    taps_rows = kern_rows.T.reshape(tap_count, views_n, 1, 1, 1)
    taps_cols = kern_cols.T.reshape(tap_count, views_n, 1, 1, 1)
    flipped_rows = kern_rows[:, ::-1].T.reshape(tap_count, views_n, 1, 1, 1)
    flipped_cols = kern_cols[:, ::-1].T.reshape(tap_count, views_n, 1, 1, 1)
    fraction = (codes[:, :, 0].astype(jnp.float32) / 16.0)[:, None, :, None, None]
    block_ids = jnp.arange(blocks_n, dtype=jnp.int32)
    same_shift = shifts[:, :, None] == shifts[:, None, :]
    earlier = block_ids[None, None, :] < block_ids[None, :, None]
    slot_rank = jnp.sum((same_shift & earlier).astype(jnp.int32), axis=2)
    peer_ids = jnp.arange(groups, dtype=jnp.int32)
    slot_ids = jnp.arange(capacity, dtype=jnp.int32)
    source_peer = (column + shifts) % groups
    target_peer = (column - shifts) % groups
    send_hot = (
        (peer_ids[None, :, None, None] == target_peer[:, None, None, :])
        & (slot_ids[None, None, :, None] == slot_rank[:, None, None, :])
    ).astype(jnp.float32)
    recv_hot = (
        (peer_ids[None, None, :, None] == source_peer[:, :, None, None])
        & (slot_ids[None, None, None, :] == slot_rank[:, :, None, None])
    ).astype(jnp.float32)
    for sweep in range(ITERS):
        blocked = estimate.reshape(depth, blocks_n, block_rows, tile_cols)
        outgoing = jnp.einsum("vpqk,zkrw->pvqzrw", send_hot, blocked, precision=highest)
        arriving = lax.all_to_all(outgoing, "gy", split_axis=0, concat_axis=0, tiled=True)
        view_blocks = jnp.einsum("vkpq,pvqzrw->vzkrw", recv_hot, arriving, precision=highest)
        view_est = shift_in(view_blocks, fraction).reshape(views_n, depth, tile_rows, tile_cols)
        padded = with_halo(view_est, (("gx", 2), ("gy", 3)), half)
        rows_done = smooth_rows(padded, taps_rows, tile_rows)
        blurred = smooth_cols(rows_done, taps_cols, tile_cols)
        ratio = views.astype(jnp.float32) / blurred
        padded_ratio = with_halo(ratio, (("gx", 2), ("gy", 3)), half)
        rows_back = smooth_rows(padded_ratio, flipped_rows, tile_rows)
        back = smooth_cols(rows_back, flipped_cols, tile_cols)
        returned = shift_back(
            back.reshape(views_n, depth, blocks_n, block_rows, tile_cols), fraction
        )
        leaving = jnp.einsum("vkpq,vzkrw->pvqzrw", recv_hot, returned, precision=highest)
        coming = lax.all_to_all(leaving, "gy", split_axis=0, concat_axis=0, tiled=True)
        summed = jnp.einsum("vpqk,pvqzrw->zkrw", send_hot, coming, precision=highest)
        estimate = estimate * (summed.reshape(depth, tile_rows, tile_cols) / views_n)
    return estimate


def split(value):
    high = value.astype(BF16)
    return high, (value - high.astype(F32)).astype(BF16)


def store_terms(ref, rows, cols, axis, step, value):
    high, low = split(value)
    for k, part in enumerate((high, high, low)):
        if axis == 0:
            ref[pl.ds(rows + k * step, value.shape[0]), pl.ds(cols, value.shape[1])] = part
        else:
            ref[pl.ds(rows, value.shape[0]), pl.ds(cols + k * step, value.shape[1])] = part


def terms(value, axis):
    high, low = split(value)
    return jnp.concatenate([high, low, high], axis=axis)


def product(left, right):
    return lax.dot_general(left, right, (((1,), (0,)), ((), ())), preferred_element_type=F32)


def rows_by(band, field):
    return product(band[...], terms(field, 0))


def cols_by(field, band):
    width = band.shape[1] // 2
    rows = field.shape[0]
    count = field.shape[1] // width - 1
    windows = [field[:, j * width : (j + 2) * width] for j in range(count)]
    done = product(terms(jnp.concatenate(windows, axis=0), 1), band[...])
    done = [done[j * rows : (j + 1) * rows] for j in range(count)]
    lane = lax.broadcasted_iota(jnp.int32, (rows, width), 1)
    tiles = [done[0][:, :width]]
    for j in range(count - 1):
        tiles.append(jnp.where(lane < width // 2, done[j][:, width:], done[j + 1][:, :width]))
    tiles.append(done[-1][:, width:])
    return tiles


def taps_of(ref, view):
    taps = [ref[view, t] for t in range(ref.shape[1])]
    return taps, functools.reduce(lambda a, b: a + b, taps)


def banded(taps, total, offset):
    value = jnp.zeros(offset.shape, F32)
    for t, tap in enumerate(taps):
        value = jnp.where(offset == t, tap, value)
    return value / jnp.full(offset.shape, total, F32)


def kernel(
    gx_n, gy_n, est_hbm, views_hbm, shifts_hbm, codes_hbm, psf_rows_hbm, psf_cols_hbm, out_ref,
    est_ref, views_ref, shifts_ref, codes_ref, psf_rows_ref, psf_cols_ref, meta_wide, meta_ref,
    est_band, views_out, views_band, meta_band, lines, frac_full, shift_full, out_own, out_in,
    band_fwd, band_back, cols_fwd, cols_back,
    local, gather_s, gather_r, halo_s, halo_r, views_s, views_r, near_s, near_r,
    meta_s, meta_r, edge_s, edge_r, out_s, out_r,
):
    views_n, depth, _, width = views_ref.shape
    blocks_n, block_rows = est_ref.shape[1:3]
    part_n = blocks_n // 2
    part_rows = part_n * block_rows
    band_rows = (part_n + 2 * HALO) * block_rows
    near_rows = (part_n + 2 * NEAR) * block_rows
    half = psf_rows_ref.shape[1] // 2
    g = lax.axis_index("gx")
    c = lax.axis_index("gy")

    def place_of(device):
        return device // 2, lax.rem(device + g, 2)

    plane, h = place_of(c)
    peers = [lax.rem(c + k, gy_n) for k in range(1, gy_n)]
    partner = {"gy": c + 1 - 2 * lax.rem(c, 2)}
    beside = {"gx": lax.rem(g - 1 + 2 * h + gx_n, gx_n)}
    pending = []

    def send(src, dst, send_sem, recv_sem, target):
        copy = pltpu.make_async_remote_copy(
            src_ref=src, dst_ref=dst, send_sem=send_sem, recv_sem=recv_sem,
            device_id=target, device_id_type=MESH,
        )
        copy.start()
        pending.append(copy)
        return copy

    loads = [
        pltpu.make_async_copy(src, dst, local.at[k])
        for k, (src, dst) in enumerate(
            (
                (codes_hbm, codes_ref), (shifts_hbm, shifts_ref), (est_hbm, est_ref),
                (views_hbm, views_ref), (psf_rows_hbm, psf_rows_ref), (psf_cols_hbm, psf_cols_ref),
            )
        )
    ]
    for load in loads:
        load.start()
    barrier = pltpu.get_barrier_semaphore()
    for target in [{"gy": p} for p in peers] + [beside]:
        pl.semaphore_signal(barrier, inc=1, device_id=target, device_id_type=MESH)
    meta_wide[...] = jnp.zeros(meta_wide.shape, F32)
    for load in loads[:2]:
        load.wait()
    meta_wide[pl.ds(0, views_n), pl.ds(0, blocks_n)] = codes_ref[...].astype(F32) / 16.0
    meta_wide[pl.ds(views_n, views_n), pl.ds(0, blocks_n)] = shifts_ref[...].astype(F32)
    meta_ref[...] = meta_wide[...].T[:blocks_n].reshape(meta_ref.shape)
    loads[2].wait()
    pl.semaphore_wait(barrier, gy_n)

    meta_copies = [
        send(meta_ref, meta_band.at[c, pl.ds(1, 2)], meta_s.at[k], meta_r.at[k], {"gy": p})
        for k, p in enumerate(peers)
    ]
    est_n = part_n + HALO
    view_n = part_n + NEAR
    gathers = []
    for k, p in enumerate(peers):
        layer, other = place_of(p)
        gathers.append(
            send(
                est_ref.at[layer, pl.ds(HALO * other, est_n)],
                est_band.at[0, c, pl.ds(HALO - HALO * other, est_n)],
                gather_s.at[k], gather_r.at[k], {"gy": p},
            )
        )
    loads[3].wait()
    view_copies = []
    for view in range(views_n):
        for layer in range(depth):
            views_out[view, layer] = (
                views_ref[view, layer].astype(F32).reshape(blocks_n, block_rows, width)
            )
        copies = []
        for k, p in enumerate(peers):
            layer, other = place_of(p)
            copies.append(
                send(
                    views_out.at[view, layer, pl.ds((part_n - NEAR) * other, view_n)],
                    views_band.at[view, c, pl.ds(NEAR - NEAR * other, view_n)],
                    views_s.at[view, k], views_r.at[view, k], {"gy": p},
                )
            )
        view_copies.append(copies)
    meta_band[c, pl.ds(1, 2)] = meta_ref[...]
    est_band[0, c, pl.ds(HALO - HALO * h, est_n)] = est_ref[plane, pl.ds(HALO * h, est_n)]
    for view in range(views_n):
        views_band[view, c, pl.ds(NEAR - NEAR * h, view_n)] = views_out[
            view, plane, pl.ds((part_n - NEAR) * h, view_n)
        ]

    for load in loads[4:]:
        load.wait()
    first_row = jnp.where((g == 0) & (h == 0), 0, -HALO * block_rows)
    last_row = jnp.where((g == gx_n - 1) & (h == 1), part_rows, part_rows + HALO * block_rows)
    for view in range(views_n):
        taps, total = taps_of(psf_rows_ref, view)
        row = lax.broadcasted_iota(jnp.int32, (near_rows, band_rows), 0) - NEAR * block_rows
        col = lax.broadcasted_iota(jnp.int32, (near_rows, band_rows), 1) - HALO * block_rows
        inside = (col >= first_row) & (col < last_row)
        outer = (row < first_row) | (row >= last_row)
        value = jnp.where(inside | outer, banded(taps, total, col - row + half), 0.0)
        store_terms(band_fwd.at[view], 0, 0, 1, band_rows, value)
        row = lax.broadcasted_iota(jnp.int32, (part_rows, near_rows), 0)
        col = lax.broadcasted_iota(jnp.int32, (part_rows, near_rows), 1) - NEAR * block_rows
        inside = (col >= first_row) & (col < last_row)
        value = jnp.where(inside, banded(taps, total, row - col + half), 0.0)
        store_terms(band_back.at[view], 0, 0, 1, near_rows, value)
        taps, total = taps_of(psf_cols_ref, view)
        for ref, sign in ((cols_fwd.at[view], 1), (cols_back.at[view], -1)):
            row = lax.broadcasted_iota(jnp.int32, (width, width), 0)
            col = lax.broadcasted_iota(jnp.int32, (width, width), 1)
            value = banded(taps, total, sign * (row - col) + half)
            store_terms(ref, 0, 0, 0, 2 * width, value)
            store_terms(ref, width, width, 0, 2 * width, value)
            row, col = row[:16], col[:16]
            blank = jnp.zeros((width - 16, width), F32)
            value = banded(taps, total, sign * (row + width - col) + half)
            value = jnp.concatenate([value, blank], axis=0)
            store_terms(ref, width, 0, 0, 2 * width, value)
            value = banded(taps, total, sign * (row - 16 - col) + half)
            value = jnp.concatenate([blank, value], axis=0)
            store_terms(ref, 0, width, 0, 2 * width, value)

    for copy in meta_copies:
        copy.wait_recv()
    edge = send(
        meta_band.at[:, 1 + h], meta_band.at[:, 3 - 3 * h], edge_s.at[0], edge_r.at[0], beside
    )
    for copy in gathers:
        copy.wait_recv()
    halo = send(
        est_band.at[0, :, pl.ds(HALO + (part_n - HALO) * h, HALO)],
        est_band.at[0, :, pl.ds((part_n + HALO) * (1 - h), HALO)],
        halo_s.at[0], halo_r.at[0], beside,
    )

    edge.wait_recv()
    for j in range(gy_n):
        found = meta_band[j].reshape(4 * 8, width)
        for view in range(views_n):
            lines[view, j] = jnp.broadcast_to(found[:, view : view + 1], found.shape)
            if j == 0:
                near = found[:, views_n + view : views_n + view + 1]
                lines[view, gy_n] = jnp.broadcast_to(near, found.shape)

    def spread(b, carry):
        place = pl.ds(b + 8 - HALO + part_n * h, 1)
        for view in range(views_n):
            for j in range(gy_n):
                frac_full[view, j, b] = jnp.broadcast_to(
                    lines[view, j, place, :], (block_rows, width)
                )
            shift_full[view, b] = jnp.broadcast_to(
                lines[view, gy_n, place, :], (block_rows, width)
            )
        return carry

    lax.fori_loop(0, part_n + 2 * HALO, spread, 0)
    halo.wait_recv()

    def pick(shift, tiles, first, sign):
        value = tiles[first % gy_n]
        for k in range(1, gy_n):
            value = jnp.where(shift == float(k), tiles[(first + sign * k) % gy_n], value)
        return value

    own = pl.ds(HALO, part_n)
    for sweep in range(ITERS):
        sums = None
        for view in range(views_n):
            if sweep == 0:
                for copy in view_copies[view]:
                    copy.wait_recv()
                near = send(
                    views_band.at[view, :, pl.ds(NEAR + (part_n - NEAR) * h, NEAR)],
                    views_band.at[view, :, pl.ds((part_n + NEAR) * (1 - h), NEAR)],
                    near_s.at[view], near_r.at[view], beside,
                )
            shift = shift_full[view]
            lane = lax.broadcasted_iota(jnp.int32, (band_rows, width), 1)
            tiles = [est_band[sweep, j] for j in range(gy_n)]
            parts = []
            for j in range(gy_n):
                moved = pick(shift, tiles, j, 1).reshape(band_rows, width)
                fraction = frac_full[view, j].reshape(band_rows, width)
                fraction = jnp.where(lane < width - 1, fraction, 0.0)
                following = pltpu.roll(moved, width - 1, 1)
                parts.append((1.0 - fraction) * moved + fraction * following)
            rows_done = rows_by(band_fwd.at[view], jnp.concatenate(parts, axis=1))
            blurred = cols_by(rows_done, cols_fwd.at[view])
            if sweep == 0:
                near.wait_recv()
            ratio = [
                views_band[view, j].reshape(near_rows, width) / blurred[j] for j in range(gy_n)
            ]
            rows_back = rows_by(band_back.at[view], jnp.concatenate(ratio, axis=1))
            back = cols_by(rows_back, cols_back.at[view])
            lane = lax.broadcasted_iota(jnp.int32, (part_rows, width), 1)
            returned = []
            for j in range(gy_n):
                fraction = frac_full[view, j, own].reshape(part_rows, width)
                kept = jnp.where(lane < width - 1, 1.0 - fraction, 1.0)
                passed = jnp.where(lane > 0, fraction, 0.0)
                value = kept * back[j] + passed * pltpu.roll(back[j], 1, 1)
                returned.append(value.reshape(part_n, block_rows, width))
            shift = shift_full[view, own]
            homes = [pick(shift, returned, j, -1) for j in range(gy_n)]
            sums = homes if sums is None else [a + b for a, b in zip(sums, homes)]
        updated = [est_band[sweep, j, own] * (sums[j] / views_n) for j in range(gy_n)]
        if sweep + 1 < ITERS:
            for j in range(gy_n):
                est_band[sweep + 1, j, own] = updated[j]
            band = est_band.at[sweep + 1]
            halos = [
                send(
                    band.at[:, pl.ds(part_n - (part_n - HALO) * h, HALO)],
                    band.at[:, pl.ds((part_n + HALO) * h, HALO)],
                    halo_s.at[2 * sweep + 1], halo_r.at[2 * sweep + 1], partner,
                ),
                send(
                    band.at[:, pl.ds(HALO + (part_n - HALO) * h, HALO)],
                    band.at[:, pl.ds((part_n + HALO) * (1 - h), HALO)],
                    halo_s.at[2 * sweep + 2], halo_r.at[2 * sweep + 2], beside,
                ),
            ]
            for copy in halos:
                copy.wait_recv()
    for j in range(gy_n):
        out_own[j] = updated[j]
    place = pl.ds(part_n * h, part_n)
    outs = [
        send(out_own.at[p], out_in.at[plane, place], out_s.at[k], out_r.at[k], {"gy": p})
        for k, p in enumerate(peers)
    ]
    out_in[plane, place] = out_own[c]
    for copy in outs:
        copy.wait_recv()
    out_ref[...] = out_in[...]
    for copy in pending:
        copy.wait_send()


def band_body(gx_n, gy_n, estimate, views, psf_rows, psf_cols, shifts, codes):
    views_n, depth, tile_rows, width = views.shape
    blocks_n = shifts.shape[1]
    block_rows = tile_rows // blocks_n
    part_n = blocks_n // 2
    part_rows = part_n * block_rows
    near_rows = part_rows + 2 * NEAR * block_rows
    band_rows = part_rows + 2 * HALO * block_rows
    others = gy_n - 1
    vmem = pltpu.VMEM
    dma = pltpu.SemaphoreType.DMA
    out = pl.pallas_call(
        functools.partial(kernel, gx_n, gy_n),
        out_shape=jax.ShapeDtypeStruct((depth, blocks_n, block_rows, width), F32),
        in_specs=[pl.BlockSpec(memory_space=pltpu.HBM)] * 6,
        out_specs=pl.BlockSpec(memory_space=pltpu.VMEM),
        scratch_shapes=[
            vmem((depth, blocks_n, block_rows, width), F32),
            vmem(views.shape, BF16),
            vmem(shifts.shape, jnp.int32),
            vmem((views_n, blocks_n), jnp.int32),
            pltpu.SMEM(psf_rows.shape, F32),
            pltpu.SMEM(psf_cols.shape, F32),
            vmem((width, width), F32),
            vmem((2, 8, width), F32),
            vmem((ITERS, gy_n, part_n + 2 * HALO, block_rows, width), F32),
            vmem((views_n, depth, blocks_n, block_rows, width), F32),
            vmem((views_n, gy_n, part_n + 2 * NEAR, block_rows, width), F32),
            vmem((gy_n, 4, 8, width), F32),
            vmem((views_n, gy_n + 1, 4 * 8, width), F32),
            vmem((views_n, gy_n, part_n + 2 * HALO, block_rows, width), F32),
            vmem((views_n, part_n + 2 * HALO, block_rows, width), F32),
            vmem((gy_n, part_n, block_rows, width), F32),
            vmem((depth, blocks_n, block_rows, width), F32),
            vmem((views_n, near_rows, 3 * band_rows), BF16),
            vmem((views_n, part_rows, 3 * near_rows), BF16),
            vmem((views_n, 6 * width, 2 * width), BF16),
            vmem((views_n, 6 * width, 2 * width), BF16),
            dma((6,)),
            dma((others,)), dma((others,)),
            dma((2 * ITERS - 1,)), dma((2 * ITERS - 1,)),
            dma((views_n, others)), dma((views_n, others)),
            dma((views_n,)), dma((views_n,)),
            dma((others,)), dma((others,)),
            dma((1,)), dma((1,)),
            dma((others,)), dma((others,)),
        ],
        compiler_params=pltpu.CompilerParams(
            collective_id=0, has_side_effects=True, vmem_limit_bytes=60 * 1024 * 1024
        ),
    )(
        estimate.reshape(depth, blocks_n, block_rows, width), views, shifts,
        codes.reshape(views_n, blocks_n), psf_rows, psf_cols,
    )
    return out.reshape(depth, tile_rows, width)


def solution(mesh):
    placed = (
        P(None, "gx", "gy"),
        P(None, None, "gx", "gy"),
        P(),
        P(),
        P(None, "gx"),
        P(None, "gx", "gy"),
    )
    gx_n, gy_n = mesh.shape["gx"], mesh.shape["gy"]

    def body(estimate, views, *rest):
        parts_n = 2 * estimate.shape[0]
        if gy_n == parts_n and gx_n % 2 == 0 and rest[2].shape[1] == 16:
            return band_body(gx_n, gy_n, estimate, views, *rest)
        return tile_body(estimate, views, *rest)

    return jax.shard_map(
        body, mesh=mesh, in_specs=placed, out_specs=P(None, "gx", "gy"), check_vma=False
    )
```

```python
import functools

import jax
import jax.numpy as jnp
from jax import lax
from jax.experimental import pallas as pl
from jax.experimental.pallas import tpu as pltpu
from jax.sharding import PartitionSpec as P

ITERS = 2
MESH = pl.DeviceIdType.MESH
F32 = jnp.float32
BF16 = jnp.bfloat16
HALO = 4
NEAR = 2


def with_halo(block, sides, width):
    for axis, dim in sides:
        count = lax.axis_size(axis)
        forward = [(i, i + 1) for i in range(count - 1)]
        backward = [(target, source) for source, target in forward]
        low = lax.ppermute(
            lax.slice_in_dim(block, block.shape[dim] - width, None, axis=dim), axis, forward
        )
        high = lax.ppermute(lax.slice_in_dim(block, 0, width, axis=dim), axis, backward)
        block = jnp.concatenate([low, block, high], axis=dim)
    return block


def shift_in(values, fraction):
    last = values.shape[-1] - 1
    column = lax.broadcasted_iota(jnp.int32, values.shape, values.ndim - 1)
    following = jnp.concatenate([values[..., 1:], values[..., -1:]], axis=-1)
    return jnp.where(column < last, (1.0 - fraction) * values + fraction * following, values)


def shift_back(values, fraction):
    last = values.shape[-1] - 1
    column = lax.broadcasted_iota(jnp.int32, values.shape, values.ndim - 1)
    preceding = jnp.concatenate([jnp.zeros_like(values[..., :1]), values[..., :-1]], axis=-1)
    own_part = jnp.where(column < last, (1.0 - fraction) * values, values)
    return own_part + fraction * preceding


def smooth_rows(padded, taps, count):
    total = taps[0] * padded[..., 0:count, :]
    for offset in range(1, taps.shape[0]):
        total = total + taps[offset] * padded[..., offset : offset + count, :]
    return total


def smooth_cols(padded, taps, count):
    total = taps[0] * padded[..., 0:count]
    for offset in range(1, taps.shape[0]):
        total = total + taps[offset] * padded[..., offset : offset + count]
    return total


def tile_body(estimate, views, psf_rows, psf_cols, shifts, codes):
    highest = lax.Precision.HIGHEST
    groups = lax.axis_size("gy")
    column = lax.axis_index("gy")
    views_n, depth, tile_rows, tile_cols = views.shape
    blocks_n = shifts.shape[1]
    block_rows = tile_rows // blocks_n
    capacity = 1 + (blocks_n + groups - 2) // groups
    tap_count = psf_rows.shape[1]
    half = tap_count // 2
    kern_rows = psf_rows / jnp.sum(psf_rows, axis=1, keepdims=True)
    kern_cols = psf_cols / jnp.sum(psf_cols, axis=1, keepdims=True)
    taps_rows = kern_rows.T.reshape(tap_count, views_n, 1, 1, 1)
    taps_cols = kern_cols.T.reshape(tap_count, views_n, 1, 1, 1)
    flipped_rows = kern_rows[:, ::-1].T.reshape(tap_count, views_n, 1, 1, 1)
    flipped_cols = kern_cols[:, ::-1].T.reshape(tap_count, views_n, 1, 1, 1)
    fraction = (codes[:, :, 0].astype(jnp.float32) / 16.0)[:, None, :, None, None]
    block_ids = jnp.arange(blocks_n, dtype=jnp.int32)
    same_shift = shifts[:, :, None] == shifts[:, None, :]
    earlier = block_ids[None, None, :] < block_ids[None, :, None]
    slot_rank = jnp.sum((same_shift & earlier).astype(jnp.int32), axis=2)
    peer_ids = jnp.arange(groups, dtype=jnp.int32)
    slot_ids = jnp.arange(capacity, dtype=jnp.int32)
    source_peer = (column + shifts) % groups
    target_peer = (column - shifts) % groups
    send_hot = (
        (peer_ids[None, :, None, None] == target_peer[:, None, None, :])
        & (slot_ids[None, None, :, None] == slot_rank[:, None, None, :])
    ).astype(jnp.float32)
    recv_hot = (
        (peer_ids[None, None, :, None] == source_peer[:, :, None, None])
        & (slot_ids[None, None, None, :] == slot_rank[:, :, None, None])
    ).astype(jnp.float32)
    for sweep in range(ITERS):
        blocked = estimate.reshape(depth, blocks_n, block_rows, tile_cols)
        outgoing = jnp.einsum("vpqk,zkrw->pvqzrw", send_hot, blocked, precision=highest)
        arriving = lax.all_to_all(outgoing, "gy", split_axis=0, concat_axis=0, tiled=True)
        view_blocks = jnp.einsum("vkpq,pvqzrw->vzkrw", recv_hot, arriving, precision=highest)
        view_est = shift_in(view_blocks, fraction).reshape(views_n, depth, tile_rows, tile_cols)
        padded = with_halo(view_est, (("gx", 2), ("gy", 3)), half)
        rows_done = smooth_rows(padded, taps_rows, tile_rows)
        blurred = smooth_cols(rows_done, taps_cols, tile_cols)
        ratio = views.astype(jnp.float32) / blurred
        padded_ratio = with_halo(ratio, (("gx", 2), ("gy", 3)), half)
        rows_back = smooth_rows(padded_ratio, flipped_rows, tile_rows)
        back = smooth_cols(rows_back, flipped_cols, tile_cols)
        returned = shift_back(
            back.reshape(views_n, depth, blocks_n, block_rows, tile_cols), fraction
        )
        leaving = jnp.einsum("vkpq,vzkrw->pvqzrw", recv_hot, returned, precision=highest)
        coming = lax.all_to_all(leaving, "gy", split_axis=0, concat_axis=0, tiled=True)
        summed = jnp.einsum("vpqk,pvqzrw->zkrw", send_hot, coming, precision=highest)
        estimate = estimate * (summed.reshape(depth, tile_rows, tile_cols) / views_n)
    return estimate


def split(value):
    high = value.astype(BF16)
    return high, (value - high.astype(F32)).astype(BF16)


def store_terms(ref, rows, cols, axis, step, value):
    high, low = split(value)
    for k, part in enumerate((high, high, low)):
        if axis == 0:
            ref[pl.ds(rows + k * step, value.shape[0]), pl.ds(cols, value.shape[1])] = part
        else:
            ref[pl.ds(rows, value.shape[0]), pl.ds(cols + k * step, value.shape[1])] = part


def terms(value, axis):
    high, low = split(value)
    return jnp.concatenate([high, low, high], axis=axis)


def product(left, right):
    return lax.dot_general(left, right, (((1,), (0,)), ((), ())), preferred_element_type=F32)


def rows_by(band, field):
    return product(band[...], terms(field, 0))


def cols_by(field, band):
    width = band.shape[1] // 2
    rows = field.shape[0]
    count = field.shape[1] // width - 1
    windows = [field[:, j * width : (j + 2) * width] for j in range(count)]
    done = product(terms(jnp.concatenate(windows, axis=0), 1), band[...])
    done = [done[j * rows : (j + 1) * rows] for j in range(count)]
    lane = lax.broadcasted_iota(jnp.int32, (rows, width), 1)
    tiles = [done[0][:, :width]]
    for j in range(count - 1):
        tiles.append(jnp.where(lane < width // 2, done[j][:, width:], done[j + 1][:, :width]))
    tiles.append(done[-1][:, width:])
    return tiles


def taps_of(ref, view):
    taps = [ref[view, t] for t in range(ref.shape[1])]
    return taps, functools.reduce(lambda a, b: a + b, taps)


def banded(taps, total, offset):
    value = jnp.zeros(offset.shape, F32)
    for t, tap in enumerate(taps):
        value = jnp.where(offset == t, tap, value)
    return value / jnp.full(offset.shape, total, F32)


def kernel(
    gx_n, gy_n, est_hbm, views_hbm, shifts_hbm, codes_hbm, psf_rows_hbm, psf_cols_hbm, out_ref,
    est_ref, views_ref, shifts_ref, codes_ref, psf_rows_ref, psf_cols_ref, meta_wide, meta_ref,
    est_band, views_out, views_band, meta_band, lines, frac_full, shift_full, out_own, out_in,
    band_fwd, band_back, cols_fwd, cols_back,
    local, gather_s, gather_r, halo_s, halo_r, views_s, views_r, near_s, near_r,
    meta_s, meta_r, edge_s, edge_r, out_s, out_r,
):
    views_n, depth, _, width = views_ref.shape
    blocks_n, block_rows = est_ref.shape[1:3]
    part_n = blocks_n // 2
    part_rows = part_n * block_rows
    band_rows = (part_n + 2 * HALO) * block_rows
    near_rows = (part_n + 2 * NEAR) * block_rows
    half = psf_rows_ref.shape[1] // 2
    g = lax.axis_index("gx")
    c = lax.axis_index("gy")

    def place_of(device):
        return device // 2, lax.rem(device + g, 2)

    plane, h = place_of(c)
    peers = [lax.rem(c + k, gy_n) for k in range(1, gy_n)]
    partner = {"gy": c + 1 - 2 * lax.rem(c, 2)}
    beside = {"gx": lax.rem(g - 1 + 2 * h + gx_n, gx_n)}
    pending = []

    def send(src, dst, send_sem, recv_sem, target):
        copy = pltpu.make_async_remote_copy(
            src_ref=src, dst_ref=dst, send_sem=send_sem, recv_sem=recv_sem,
            device_id=target, device_id_type=MESH,
        )
        copy.start()
        pending.append(copy)
        return copy

    loads = [
        pltpu.make_async_copy(src, dst, local.at[k])
        for k, (src, dst) in enumerate(
            (
                (codes_hbm, codes_ref), (shifts_hbm, shifts_ref), (est_hbm, est_ref),
                (views_hbm, views_ref), (psf_rows_hbm, psf_rows_ref), (psf_cols_hbm, psf_cols_ref),
            )
        )
    ]
    for load in loads:
        load.start()
    barrier = pltpu.get_barrier_semaphore()
    for target in [{"gy": p} for p in peers] + [beside]:
        pl.semaphore_signal(barrier, inc=1, device_id=target, device_id_type=MESH)
    meta_wide[...] = jnp.zeros(meta_wide.shape, F32)
    for load in loads[:2]:
        load.wait()
    meta_wide[pl.ds(0, views_n), pl.ds(0, blocks_n)] = codes_ref[...].astype(F32) / 16.0
    meta_wide[pl.ds(views_n, views_n), pl.ds(0, blocks_n)] = shifts_ref[...].astype(F32)
    meta_ref[...] = meta_wide[...].T[:blocks_n].reshape(meta_ref.shape)
    loads[2].wait()
    pl.semaphore_wait(barrier, gy_n)

    meta_copies = [
        send(meta_ref, meta_band.at[c, pl.ds(1, 2)], meta_s.at[k], meta_r.at[k], {"gy": p})
        for k, p in enumerate(peers)
    ]
    est_n = part_n + HALO
    gathers = []
    for k, p in enumerate(peers):
        layer, other = place_of(p)
        gathers.append(
            send(
                est_ref.at[layer, pl.ds(HALO * other, est_n)],
                est_band.at[0, c, pl.ds(HALO - HALO * other, est_n)],
                gather_s.at[k], gather_r.at[k], {"gy": p},
            )
        )
    loads[3].wait()
    for view in range(views_n):
        for layer in range(depth):
            views_out[view, layer] = (
                views_ref[view, layer].astype(F32).reshape(blocks_n, block_rows, width)
            )
    seen = pl.ds(NEAR, part_n)
    view_copies = []

    def send_view(view):
        copies = []
        for k, p in enumerate(peers):
            layer, other = place_of(p)
            copies.append(
                send(
                    views_out.at[view, layer, pl.ds(part_n * other, part_n)],
                    views_band.at[view, c, seen],
                    views_s.at[view, k], views_r.at[view, k], {"gy": p},
                )
            )
        view_copies.append(copies)

    send_view(0)
    meta_band[c, pl.ds(1, 2)] = meta_ref[...]
    est_band[0, c, pl.ds(HALO - HALO * h, est_n)] = est_ref[plane, pl.ds(HALO * h, est_n)]
    for view in range(views_n):
        views_band[view, c, seen] = views_out[view, plane, pl.ds(part_n * h, part_n)]

    for load in loads[4:]:
        load.wait()
    first_row = jnp.where((g == 0) & (h == 0), 0, -HALO * block_rows)
    last_row = jnp.where((g == gx_n - 1) & (h == 1), part_rows, part_rows + HALO * block_rows)
    for view in range(views_n):
        taps, total = taps_of(psf_rows_ref, view)
        row = lax.broadcasted_iota(jnp.int32, (near_rows, band_rows), 0) - NEAR * block_rows
        col = lax.broadcasted_iota(jnp.int32, (near_rows, band_rows), 1) - HALO * block_rows
        inside = (col >= first_row) & (col < last_row)
        outer = (row < first_row) | (row >= last_row)
        value = jnp.where(inside | outer, banded(taps, total, col - row + half), 0.0)
        store_terms(band_fwd.at[view], 0, 0, 1, band_rows, value)
        row = lax.broadcasted_iota(jnp.int32, (part_rows, near_rows), 0)
        col = lax.broadcasted_iota(jnp.int32, (part_rows, near_rows), 1) - NEAR * block_rows
        inside = (col >= first_row) & (col < last_row)
        value = jnp.where(inside, banded(taps, total, row - col + half), 0.0)
        store_terms(band_back.at[view], 0, 0, 1, near_rows, value)
        taps, total = taps_of(psf_cols_ref, view)
        for ref, sign in ((cols_fwd.at[view], 1), (cols_back.at[view], -1)):
            row = lax.broadcasted_iota(jnp.int32, (width, width), 0)
            col = lax.broadcasted_iota(jnp.int32, (width, width), 1)
            value = banded(taps, total, sign * (row - col) + half)
            store_terms(ref, 0, 0, 0, 2 * width, value)
            store_terms(ref, width, width, 0, 2 * width, value)
            row, col = row[:16], col[:16]
            blank = jnp.zeros((width - 16, width), F32)
            value = banded(taps, total, sign * (row + width - col) + half)
            value = jnp.concatenate([value, blank], axis=0)
            store_terms(ref, width, 0, 0, 2 * width, value)
            value = banded(taps, total, sign * (row - 16 - col) + half)
            value = jnp.concatenate([blank, value], axis=0)
            store_terms(ref, 0, width, 0, 2 * width, value)

    for copy in meta_copies:
        copy.wait_recv()
    edge = send(
        meta_band.at[:, 1 + h], meta_band.at[:, 3 - 3 * h], edge_s.at[0], edge_r.at[0], beside
    )
    for copy in gathers:
        copy.wait_recv()
    halo = send(
        est_band.at[0, :, pl.ds(HALO + (part_n - HALO) * h, HALO)],
        est_band.at[0, :, pl.ds((part_n + HALO) * (1 - h), HALO)],
        halo_s.at[0], halo_r.at[0], beside,
    )
    send_view(1)

    edge.wait_recv()
    for j in range(gy_n):
        found = meta_band[j].reshape(4 * 8, width)
        for view in range(views_n):
            lines[view, j] = jnp.broadcast_to(found[:, view : view + 1], found.shape)
            if j == 0:
                near = found[:, views_n + view : views_n + view + 1]
                lines[view, gy_n] = jnp.broadcast_to(near, found.shape)

    def spread(b, carry):
        place = pl.ds(b + 8 - HALO + part_n * h, 1)
        for view in range(views_n):
            for j in range(gy_n):
                frac_full[view, j, b] = jnp.broadcast_to(
                    lines[view, j, place, :], (block_rows, width)
                )
            shift_full[view, b] = jnp.broadcast_to(
                lines[view, gy_n, place, :], (block_rows, width)
            )
        return carry

    lax.fori_loop(0, part_n + 2 * HALO, spread, 0)
    halo.wait_recv()

    def pick(shift, tiles, first, sign):
        value = tiles[first % gy_n]
        for k in range(1, gy_n):
            value = jnp.where(shift == float(k), tiles[(first + sign * k) % gy_n], value)
        return value

    own = pl.ds(HALO, part_n)
    for sweep in range(ITERS):
        sums = None
        for view in range(views_n):
            if sweep == 0:
                for copy in view_copies[view]:
                    copy.wait_recv()
                band = views_band.at[view]
                nears = [
                    send(
                        band.at[:, pl.ds(part_n - (part_n - NEAR) * h, NEAR)],
                        band.at[:, pl.ds((part_n + NEAR) * h, NEAR)],
                        near_s.at[view, 0], near_r.at[view, 0], partner,
                    ),
                    send(
                        band.at[:, pl.ds(NEAR + (part_n - NEAR) * h, NEAR)],
                        band.at[:, pl.ds((part_n + NEAR) * (1 - h), NEAR)],
                        near_s.at[view, 1], near_r.at[view, 1], beside,
                    ),
                ]
                if view + 2 < views_n:
                    send_view(view + 2)
            shift = shift_full[view]
            lane = lax.broadcasted_iota(jnp.int32, (band_rows, width), 1)
            tiles = [est_band[sweep, j] for j in range(gy_n)]
            parts = []
            for j in range(gy_n):
                moved = pick(shift, tiles, j, 1).reshape(band_rows, width)
                fraction = frac_full[view, j].reshape(band_rows, width)
                fraction = jnp.where(lane < width - 1, fraction, 0.0)
                following = pltpu.roll(moved, width - 1, 1)
                parts.append((1.0 - fraction) * moved + fraction * following)
            rows_done = rows_by(band_fwd.at[view], jnp.concatenate(parts, axis=1))
            blurred = cols_by(rows_done, cols_fwd.at[view])
            if sweep == 0:
                for copy in nears:
                    copy.wait_recv()
            ratio = [
                views_band[view, j].reshape(near_rows, width) / blurred[j] for j in range(gy_n)
            ]
            rows_back = rows_by(band_back.at[view], jnp.concatenate(ratio, axis=1))
            back = cols_by(rows_back, cols_back.at[view])
            lane = lax.broadcasted_iota(jnp.int32, (part_rows, width), 1)
            returned = []
            for j in range(gy_n):
                fraction = frac_full[view, j, own].reshape(part_rows, width)
                kept = jnp.where(lane < width - 1, 1.0 - fraction, 1.0)
                passed = jnp.where(lane > 0, fraction, 0.0)
                value = kept * back[j] + passed * pltpu.roll(back[j], 1, 1)
                returned.append(value.reshape(part_n, block_rows, width))
            shift = shift_full[view, own]
            homes = [pick(shift, returned, j, -1) for j in range(gy_n)]
            sums = homes if sums is None else [a + b for a, b in zip(sums, homes)]
        updated = [est_band[sweep, j, own] * (sums[j] / views_n) for j in range(gy_n)]
        if sweep + 1 < ITERS:
            for j in range(gy_n):
                est_band[sweep + 1, j, own] = updated[j]
            band = est_band.at[sweep + 1]
            halos = [
                send(
                    band.at[:, pl.ds(part_n - (part_n - HALO) * h, HALO)],
                    band.at[:, pl.ds((part_n + HALO) * h, HALO)],
                    halo_s.at[2 * sweep + 1], halo_r.at[2 * sweep + 1], partner,
                ),
                send(
                    band.at[:, pl.ds(HALO + (part_n - HALO) * h, HALO)],
                    band.at[:, pl.ds((part_n + HALO) * (1 - h), HALO)],
                    halo_s.at[2 * sweep + 2], halo_r.at[2 * sweep + 2], beside,
                ),
            ]
            for copy in halos:
                copy.wait_recv()
    for j in range(gy_n):
        out_own[j] = updated[j]
    place = pl.ds(part_n * h, part_n)
    outs = [
        send(out_own.at[p], out_in.at[plane, place], out_s.at[k], out_r.at[k], {"gy": p})
        for k, p in enumerate(peers)
    ]
    out_in[plane, place] = out_own[c]
    for copy in outs:
        copy.wait_recv()
    out_ref[...] = out_in[...]
    for copy in pending:
        copy.wait_send()


def band_body(gx_n, gy_n, estimate, views, psf_rows, psf_cols, shifts, codes):
    views_n, depth, tile_rows, width = views.shape
    blocks_n = shifts.shape[1]
    block_rows = tile_rows // blocks_n
    part_n = blocks_n // 2
    part_rows = part_n * block_rows
    near_rows = part_rows + 2 * NEAR * block_rows
    band_rows = part_rows + 2 * HALO * block_rows
    others = gy_n - 1
    vmem = pltpu.VMEM
    dma = pltpu.SemaphoreType.DMA
    out = pl.pallas_call(
        functools.partial(kernel, gx_n, gy_n),
        out_shape=jax.ShapeDtypeStruct((depth, blocks_n, block_rows, width), F32),
        in_specs=[pl.BlockSpec(memory_space=pltpu.HBM)] * 6,
        out_specs=pl.BlockSpec(memory_space=pltpu.VMEM),
        scratch_shapes=[
            vmem((depth, blocks_n, block_rows, width), F32),
            vmem(views.shape, BF16),
            vmem(shifts.shape, jnp.int32),
            vmem((views_n, blocks_n), jnp.int32),
            pltpu.SMEM(psf_rows.shape, F32),
            pltpu.SMEM(psf_cols.shape, F32),
            vmem((width, width), F32),
            vmem((2, 8, width), F32),
            vmem((ITERS, gy_n, part_n + 2 * HALO, block_rows, width), F32),
            vmem((views_n, depth, blocks_n, block_rows, width), F32),
            vmem((views_n, gy_n, part_n + 2 * NEAR, block_rows, width), F32),
            vmem((gy_n, 4, 8, width), F32),
            vmem((views_n, gy_n + 1, 4 * 8, width), F32),
            vmem((views_n, gy_n, part_n + 2 * HALO, block_rows, width), F32),
            vmem((views_n, part_n + 2 * HALO, block_rows, width), F32),
            vmem((gy_n, part_n, block_rows, width), F32),
            vmem((depth, blocks_n, block_rows, width), F32),
            vmem((views_n, near_rows, 3 * band_rows), BF16),
            vmem((views_n, part_rows, 3 * near_rows), BF16),
            vmem((views_n, 6 * width, 2 * width), BF16),
            vmem((views_n, 6 * width, 2 * width), BF16),
            dma((6,)),
            dma((others,)), dma((others,)),
            dma((2 * ITERS - 1,)), dma((2 * ITERS - 1,)),
            dma((views_n, others)), dma((views_n, others)),
            dma((views_n, 2)), dma((views_n, 2)),
            dma((others,)), dma((others,)),
            dma((1,)), dma((1,)),
            dma((others,)), dma((others,)),
        ],
        compiler_params=pltpu.CompilerParams(
            collective_id=0, has_side_effects=True, vmem_limit_bytes=60 * 1024 * 1024
        ),
    )(
        estimate.reshape(depth, blocks_n, block_rows, width), views, shifts,
        codes.reshape(views_n, blocks_n), psf_rows, psf_cols,
    )
    return out.reshape(depth, tile_rows, width)


def solution(mesh):
    placed = (
        P(None, "gx", "gy"),
        P(None, None, "gx", "gy"),
        P(),
        P(),
        P(None, "gx"),
        P(None, "gx", "gy"),
    )
    gx_n, gy_n = mesh.shape["gx"], mesh.shape["gy"]

    def body(estimate, views, *rest):
        parts_n = 2 * estimate.shape[0]
        if gy_n == parts_n and gx_n % 2 == 0 and rest[2].shape[1] == 16:
            return band_body(gx_n, gy_n, estimate, views, *rest)
        return tile_body(estimate, views, *rest)

    return jax.shard_map(
        body, mesh=mesh, in_specs=placed, out_specs=P(None, "gx", "gy"), check_vma=False
    )
```

```python
import functools

import jax
import jax.numpy as jnp
from jax import lax
from jax.experimental import pallas as pl
from jax.experimental.pallas import tpu as pltpu
from jax.sharding import PartitionSpec as P

ITERS = 2
MESH = pl.DeviceIdType.MESH
F32 = jnp.float32
BF16 = jnp.bfloat16
HALO = 4
NEAR = 2


def with_halo(block, sides, width):
    for axis, dim in sides:
        count = lax.axis_size(axis)
        forward = [(i, i + 1) for i in range(count - 1)]
        backward = [(target, source) for source, target in forward]
        low = lax.ppermute(
            lax.slice_in_dim(block, block.shape[dim] - width, None, axis=dim), axis, forward
        )
        high = lax.ppermute(lax.slice_in_dim(block, 0, width, axis=dim), axis, backward)
        block = jnp.concatenate([low, block, high], axis=dim)
    return block


def shift_in(values, fraction):
    last = values.shape[-1] - 1
    column = lax.broadcasted_iota(jnp.int32, values.shape, values.ndim - 1)
    following = jnp.concatenate([values[..., 1:], values[..., -1:]], axis=-1)
    return jnp.where(column < last, (1.0 - fraction) * values + fraction * following, values)


def shift_back(values, fraction):
    last = values.shape[-1] - 1
    column = lax.broadcasted_iota(jnp.int32, values.shape, values.ndim - 1)
    preceding = jnp.concatenate([jnp.zeros_like(values[..., :1]), values[..., :-1]], axis=-1)
    own_part = jnp.where(column < last, (1.0 - fraction) * values, values)
    return own_part + fraction * preceding


def smooth_rows(padded, taps, count):
    total = taps[0] * padded[..., 0:count, :]
    for offset in range(1, taps.shape[0]):
        total = total + taps[offset] * padded[..., offset : offset + count, :]
    return total


def smooth_cols(padded, taps, count):
    total = taps[0] * padded[..., 0:count]
    for offset in range(1, taps.shape[0]):
        total = total + taps[offset] * padded[..., offset : offset + count]
    return total


def tile_body(estimate, views, psf_rows, psf_cols, shifts, codes):
    highest = lax.Precision.HIGHEST
    groups = lax.axis_size("gy")
    column = lax.axis_index("gy")
    views_n, depth, tile_rows, tile_cols = views.shape
    blocks_n = shifts.shape[1]
    block_rows = tile_rows // blocks_n
    capacity = 1 + (blocks_n + groups - 2) // groups
    tap_count = psf_rows.shape[1]
    half = tap_count // 2
    kern_rows = psf_rows / jnp.sum(psf_rows, axis=1, keepdims=True)
    kern_cols = psf_cols / jnp.sum(psf_cols, axis=1, keepdims=True)
    taps_rows = kern_rows.T.reshape(tap_count, views_n, 1, 1, 1)
    taps_cols = kern_cols.T.reshape(tap_count, views_n, 1, 1, 1)
    flipped_rows = kern_rows[:, ::-1].T.reshape(tap_count, views_n, 1, 1, 1)
    flipped_cols = kern_cols[:, ::-1].T.reshape(tap_count, views_n, 1, 1, 1)
    fraction = (codes[:, :, 0].astype(jnp.float32) / 16.0)[:, None, :, None, None]
    block_ids = jnp.arange(blocks_n, dtype=jnp.int32)
    same_shift = shifts[:, :, None] == shifts[:, None, :]
    earlier = block_ids[None, None, :] < block_ids[None, :, None]
    slot_rank = jnp.sum((same_shift & earlier).astype(jnp.int32), axis=2)
    peer_ids = jnp.arange(groups, dtype=jnp.int32)
    slot_ids = jnp.arange(capacity, dtype=jnp.int32)
    source_peer = (column + shifts) % groups
    target_peer = (column - shifts) % groups
    send_hot = (
        (peer_ids[None, :, None, None] == target_peer[:, None, None, :])
        & (slot_ids[None, None, :, None] == slot_rank[:, None, None, :])
    ).astype(jnp.float32)
    recv_hot = (
        (peer_ids[None, None, :, None] == source_peer[:, :, None, None])
        & (slot_ids[None, None, None, :] == slot_rank[:, :, None, None])
    ).astype(jnp.float32)
    for sweep in range(ITERS):
        blocked = estimate.reshape(depth, blocks_n, block_rows, tile_cols)
        outgoing = jnp.einsum("vpqk,zkrw->pvqzrw", send_hot, blocked, precision=highest)
        arriving = lax.all_to_all(outgoing, "gy", split_axis=0, concat_axis=0, tiled=True)
        view_blocks = jnp.einsum("vkpq,pvqzrw->vzkrw", recv_hot, arriving, precision=highest)
        view_est = shift_in(view_blocks, fraction).reshape(views_n, depth, tile_rows, tile_cols)
        padded = with_halo(view_est, (("gx", 2), ("gy", 3)), half)
        rows_done = smooth_rows(padded, taps_rows, tile_rows)
        blurred = smooth_cols(rows_done, taps_cols, tile_cols)
        ratio = views.astype(jnp.float32) / blurred
        padded_ratio = with_halo(ratio, (("gx", 2), ("gy", 3)), half)
        rows_back = smooth_rows(padded_ratio, flipped_rows, tile_rows)
        back = smooth_cols(rows_back, flipped_cols, tile_cols)
        returned = shift_back(
            back.reshape(views_n, depth, blocks_n, block_rows, tile_cols), fraction
        )
        leaving = jnp.einsum("vkpq,vzkrw->pvqzrw", recv_hot, returned, precision=highest)
        coming = lax.all_to_all(leaving, "gy", split_axis=0, concat_axis=0, tiled=True)
        summed = jnp.einsum("vpqk,pvqzrw->zkrw", send_hot, coming, precision=highest)
        estimate = estimate * (summed.reshape(depth, tile_rows, tile_cols) / views_n)
    return estimate


def split(value):
    high = value.astype(BF16)
    return high, (value - high.astype(F32)).astype(BF16)


def store_terms(ref, rows, cols, axis, step, value):
    high, low = split(value)
    for k, part in enumerate((high, high, low)):
        if axis == 0:
            ref[pl.ds(rows + k * step, value.shape[0]), pl.ds(cols, value.shape[1])] = part
        else:
            ref[pl.ds(rows, value.shape[0]), pl.ds(cols + k * step, value.shape[1])] = part


def terms(value, axis):
    high, low = split(value)
    return jnp.concatenate([high, low, high], axis=axis)


def product(left, right):
    return lax.dot_general(left, right, (((1,), (0,)), ((), ())), preferred_element_type=F32)


def rows_by(band, field):
    return product(band[...], terms(field, 0))


def cols_by(field, band):
    width = band.shape[1] // 2
    rows = field.shape[0]
    count = field.shape[1] // width - 1
    windows = [field[:, j * width : (j + 2) * width] for j in range(count)]
    done = product(terms(jnp.concatenate(windows, axis=0), 1), band[...])
    done = [done[j * rows : (j + 1) * rows] for j in range(count)]
    lane = lax.broadcasted_iota(jnp.int32, (rows, width), 1)
    tiles = [done[0][:, :width]]
    for j in range(count - 1):
        tiles.append(jnp.where(lane < width // 2, done[j][:, width:], done[j + 1][:, :width]))
    tiles.append(done[-1][:, width:])
    return tiles


def taps_of(ref, view):
    taps = [ref[view, t] for t in range(ref.shape[1])]
    return taps, functools.reduce(lambda a, b: a + b, taps)


def banded(taps, total, offset):
    value = jnp.zeros(offset.shape, F32)
    for t, tap in enumerate(taps):
        value = jnp.where(offset == t, tap, value)
    return value / jnp.full(offset.shape, total, F32)


def kernel(
    gx_n, gy_n, est_hbm, views_hbm, shifts_hbm, codes_hbm, psf_rows_hbm, psf_cols_hbm, out_ref,
    est_ref, views_ref, shifts_ref, codes_ref, psf_rows_ref, psf_cols_ref, meta_wide, meta_ref,
    est_band, views_out, views_band, meta_band, lines, frac_full, shift_full, out_own, out_in,
    band_fwd, band_back, cols_fwd, cols_back,
    local, gather_s, gather_r, halo_s, halo_r, views_s, views_r, near_s, near_r,
    meta_s, meta_r, edge_s, edge_r, out_s, out_r,
):
    views_n, depth, _, width = views_ref.shape
    blocks_n, block_rows = est_ref.shape[1:3]
    part_n = blocks_n // 2
    part_rows = part_n * block_rows
    band_rows = (part_n + 2 * HALO) * block_rows
    near_rows = (part_n + 2 * NEAR) * block_rows
    half = psf_rows_ref.shape[1] // 2
    g = lax.axis_index("gx")
    c = lax.axis_index("gy")

    def place_of(device):
        return device // 2, lax.rem(device + g, 2)

    plane, h = place_of(c)
    peers = [lax.rem(c + k, gy_n) for k in range(1, gy_n)]
    partner = {"gy": c + 1 - 2 * lax.rem(c, 2)}
    beside = {"gx": lax.rem(g - 1 + 2 * h + gx_n, gx_n)}
    pending = []

    def send(src, dst, send_sem, recv_sem, target):
        copy = pltpu.make_async_remote_copy(
            src_ref=src, dst_ref=dst, send_sem=send_sem, recv_sem=recv_sem,
            device_id=target, device_id_type=MESH,
        )
        copy.start()
        pending.append(copy)
        return copy

    loads = [
        pltpu.make_async_copy(src, dst, local.at[k])
        for k, (src, dst) in enumerate(
            (
                (codes_hbm, codes_ref), (shifts_hbm, shifts_ref), (est_hbm, est_ref),
                (views_hbm, views_ref), (psf_rows_hbm, psf_rows_ref), (psf_cols_hbm, psf_cols_ref),
            )
        )
    ]
    for load in loads:
        load.start()
    barrier = pltpu.get_barrier_semaphore()
    for target in [{"gy": p} for p in peers] + [beside]:
        pl.semaphore_signal(barrier, inc=1, device_id=target, device_id_type=MESH)
    meta_wide[...] = jnp.zeros(meta_wide.shape, F32)
    for load in loads[:2]:
        load.wait()
    meta_wide[pl.ds(0, views_n), pl.ds(0, blocks_n)] = codes_ref[...].astype(F32) / 16.0
    meta_wide[pl.ds(views_n, views_n), pl.ds(0, blocks_n)] = shifts_ref[...].astype(F32)
    meta_ref[...] = meta_wide[...].T[:blocks_n].reshape(meta_ref.shape)
    loads[2].wait()
    pl.semaphore_wait(barrier, gy_n)

    meta_copies = [
        send(meta_ref, meta_band.at[c, pl.ds(1, 2)], meta_s.at[k], meta_r.at[k], {"gy": p})
        for k, p in enumerate(peers)
    ]
    est_n = part_n + HALO
    gathers = []
    for k, p in enumerate(peers):
        layer, other = place_of(p)
        gathers.append(
            send(
                est_ref.at[layer, pl.ds(HALO * other, est_n)],
                est_band.at[0, c, pl.ds(HALO - HALO * other, est_n)],
                gather_s.at[k], gather_r.at[k], {"gy": p},
            )
        )
    loads[3].wait()
    for view in range(views_n):
        for layer in range(depth):
            views_out[view, layer] = (
                views_ref[view, layer].astype(F32).reshape(blocks_n, block_rows, width)
            )
    seen = pl.ds(NEAR, part_n)
    view_copies = []

    def send_view(view):
        copies = []
        for k, p in enumerate(peers):
            layer, other = place_of(p)
            copies.append(
                send(
                    views_out.at[view, layer, pl.ds(part_n * other, part_n)],
                    views_band.at[view, c, seen],
                    views_s.at[view, k], views_r.at[view, k], {"gy": p},
                )
            )
        view_copies.append(copies)

    send_view(0)
    meta_band[c, pl.ds(1, 2)] = meta_ref[...]
    est_band[0, c, pl.ds(HALO - HALO * h, est_n)] = est_ref[plane, pl.ds(HALO * h, est_n)]
    for view in range(views_n):
        views_band[view, c, seen] = views_out[view, plane, pl.ds(part_n * h, part_n)]

    for load in loads[4:]:
        load.wait()
    first_row = jnp.where((g == 0) & (h == 0), 0, -HALO * block_rows)
    last_row = jnp.where((g == gx_n - 1) & (h == 1), part_rows, part_rows + HALO * block_rows)
    for view in range(views_n):
        taps, total = taps_of(psf_rows_ref, view)
        row = lax.broadcasted_iota(jnp.int32, (near_rows, band_rows), 0) - NEAR * block_rows
        col = lax.broadcasted_iota(jnp.int32, (near_rows, band_rows), 1) - HALO * block_rows
        inside = (col >= first_row) & (col < last_row)
        outer = (row < first_row) | (row >= last_row)
        value = jnp.where(inside | outer, banded(taps, total, col - row + half), 0.0)
        store_terms(band_fwd.at[view], 0, 0, 1, band_rows, value)
        row = lax.broadcasted_iota(jnp.int32, (part_rows, near_rows), 0)
        col = lax.broadcasted_iota(jnp.int32, (part_rows, near_rows), 1) - NEAR * block_rows
        inside = (col >= first_row) & (col < last_row)
        value = jnp.where(inside, banded(taps, total, row - col + half), 0.0)
        store_terms(band_back.at[view], 0, 0, 1, near_rows, value)
        taps, total = taps_of(psf_cols_ref, view)
        for ref, sign in ((cols_fwd.at[view], 1), (cols_back.at[view], -1)):
            row = lax.broadcasted_iota(jnp.int32, (width, width), 0)
            col = lax.broadcasted_iota(jnp.int32, (width, width), 1)
            value = banded(taps, total, sign * (row - col) + half)
            store_terms(ref, 0, 0, 0, 2 * width, value)
            store_terms(ref, width, width, 0, 2 * width, value)
            row, col = row[:16], col[:16]
            blank = jnp.zeros((width - 16, width), F32)
            value = banded(taps, total, sign * (row + width - col) + half)
            value = jnp.concatenate([value, blank], axis=0)
            store_terms(ref, width, 0, 0, 2 * width, value)
            value = banded(taps, total, sign * (row - 16 - col) + half)
            value = jnp.concatenate([blank, value], axis=0)
            store_terms(ref, 0, width, 0, 2 * width, value)

    for copy in meta_copies:
        copy.wait_recv()
    edge = send(
        meta_band.at[:, 1 + h], meta_band.at[:, 3 - 3 * h], edge_s.at[0], edge_r.at[0], beside
    )
    for copy in gathers:
        copy.wait_recv()
    halo = send(
        est_band.at[0, :, pl.ds(HALO + (part_n - HALO) * h, HALO)],
        est_band.at[0, :, pl.ds((part_n + HALO) * (1 - h), HALO)],
        halo_s.at[0], halo_r.at[0], beside,
    )
    send_view(1)

    edge.wait_recv()
    for j in range(gy_n):
        found = meta_band[j].reshape(4 * 8, width)
        for view in range(views_n):
            lines[view, j] = jnp.broadcast_to(found[:, view : view + 1], found.shape)
            if j == 0:
                near = found[:, views_n + view : views_n + view + 1]
                lines[view, gy_n] = jnp.broadcast_to(near, found.shape)

    def spread(b, carry):
        place = pl.ds(b + 8 - HALO + part_n * h, 1)
        for view in range(views_n):
            for j in range(gy_n):
                frac_full[view, j, b] = jnp.broadcast_to(
                    lines[view, j, place, :], (block_rows, width)
                )
            shift_full[view, b] = jnp.broadcast_to(
                lines[view, gy_n, place, :], (block_rows, width)
            )
        return carry

    lax.fori_loop(0, part_n + 2 * HALO, spread, 0)
    halo.wait_recv()

    def pick(shift, tiles, first, sign):
        value = tiles[first % gy_n]
        for k in range(1, gy_n):
            value = jnp.where(shift == float(k), tiles[(first + sign * k) % gy_n], value)
        return value

    own = pl.ds(HALO, part_n)

    def viewed(sweep, view, start, count):
        place = pl.ds(start, count)
        rows = count * block_rows
        shift = shift_full[view, place]
        lane = lax.broadcasted_iota(jnp.int32, (rows, width), 1)
        tiles = [est_band[sweep, j, place] for j in range(gy_n)]
        parts = []
        for j in range(gy_n):
            moved = pick(shift, tiles, j, 1).reshape(rows, width)
            fraction = frac_full[view, j, place].reshape(rows, width)
            fraction = jnp.where(lane < width - 1, fraction, 0.0)
            following = pltpu.roll(moved, width - 1, 1)
            parts.append((1.0 - fraction) * moved + fraction * following)
        return jnp.concatenate(parts, axis=1)

    def blur(sweep, views):
        fields = [viewed(sweep, view, 0, part_n + 2 * HALO) for view in views]
        fields = [rows_by(band_fwd.at[view], x) for view, x in zip(views, fields)]
        return [cols_by(x, cols_fwd.at[view]) for view, x in zip(views, fields)]

    def blur_cols_first(sweep, views, halos):
        inner = [viewed(sweep, view, HALO, part_n) for view in views]
        inner = [cols_by(x, cols_fwd.at[view]) for view, x in zip(views, inner)]
        inner = [jnp.concatenate(tiles, axis=1) for tiles in inner]
        for copy in halos:
            copy.wait_recv()
        cut = HALO * block_rows
        outer = [
            jnp.concatenate(
                [viewed(sweep, view, 0, HALO), viewed(sweep, view, HALO + part_n, HALO)], axis=0
            )
            for view in views
        ]
        outer = [cols_by(x, cols_fwd.at[view]) for view, x in zip(views, outer)]
        outer = [jnp.concatenate(tiles, axis=1) for tiles in outer]
        fields = [jnp.concatenate([o[:cut], i, o[cut:]], axis=0) for i, o in zip(inner, outer)]
        fields = [rows_by(band_fwd.at[view], x) for view, x in zip(views, fields)]
        return [[x[:, j * width : (j + 1) * width] for j in range(gy_n)] for x in fields]

    def correct(views, blurred):
        ratio = [
            [views_band[view, j].reshape(near_rows, width) / tiles[j] for j in range(gy_n)]
            for view, tiles in zip(views, blurred)
        ]
        fields = [
            rows_by(band_back.at[view], jnp.concatenate(tiles, axis=1))
            for view, tiles in zip(views, ratio)
        ]
        back = [cols_by(x, cols_back.at[view]) for view, x in zip(views, fields)]
        lane = lax.broadcasted_iota(jnp.int32, (part_rows, width), 1)
        homes = []
        for view, tiles in zip(views, back):
            returned = []
            for j in range(gy_n):
                fraction = frac_full[view, j, own].reshape(part_rows, width)
                kept = jnp.where(lane < width - 1, 1.0 - fraction, 1.0)
                passed = jnp.where(lane > 0, fraction, 0.0)
                value = kept * tiles[j] + passed * pltpu.roll(tiles[j], 1, 1)
                returned.append(value.reshape(part_n, block_rows, width))
            shift = shift_full[view, own]
            homes.append([pick(shift, returned, j, -1) for j in range(gy_n)])
        return homes

    def add_up(all_homes):
        return functools.reduce(lambda x, y: [a + b for a, b in zip(x, y)], all_homes)

    def arrive(view):
        for copy in view_copies[view]:
            copy.wait_recv()
        band = views_band.at[view]
        nears = [
            send(
                band.at[:, pl.ds(part_n - (part_n - NEAR) * h, NEAR)],
                band.at[:, pl.ds((part_n + NEAR) * h, NEAR)],
                near_s.at[view, 0], near_r.at[view, 0], partner,
            ),
            send(
                band.at[:, pl.ds(NEAR + (part_n - NEAR) * h, NEAR)],
                band.at[:, pl.ds((part_n + NEAR) * (1 - h), NEAR)],
                near_s.at[view, 1], near_r.at[view, 1], beside,
            ),
        ]
        if view + 2 < views_n:
            send_view(view + 2)
        return nears

    for sweep in range(ITERS):
        if sweep == 0:
            nears = []
            blurred = []
            for view in range(0, views_n, 2):
                blurred += blur(sweep, list(range(view, min(view + 2, views_n))))
                nears.append(arrive(view // 2))
            homes = []
            for view in range(views_n):
                if len(nears) < min(view + 2, views_n):
                    nears.append(arrive(len(nears)))
                for copy in nears[view]:
                    copy.wait_recv()
                homes += correct([view], [blurred[view]])
        else:
            every = list(range(views_n))
            homes = correct(every, blur_cols_first(sweep, every, halos))
        sums = add_up(homes)
        updated = [est_band[sweep, j, own] * (sums[j] / views_n) for j in range(gy_n)]
        if sweep + 1 < ITERS:
            for j in range(gy_n):
                est_band[sweep + 1, j, own] = updated[j]
            band = est_band.at[sweep + 1]
            halos = [
                send(
                    band.at[:, pl.ds(part_n - (part_n - HALO) * h, HALO)],
                    band.at[:, pl.ds((part_n + HALO) * h, HALO)],
                    halo_s.at[2 * sweep + 1], halo_r.at[2 * sweep + 1], partner,
                ),
                send(
                    band.at[:, pl.ds(HALO + (part_n - HALO) * h, HALO)],
                    band.at[:, pl.ds((part_n + HALO) * (1 - h), HALO)],
                    halo_s.at[2 * sweep + 2], halo_r.at[2 * sweep + 2], beside,
                ),
            ]
    for j in range(gy_n):
        out_own[j] = updated[j]
    place = pl.ds(part_n * h, part_n)
    outs = [
        send(out_own.at[p], out_in.at[plane, place], out_s.at[k], out_r.at[k], {"gy": p})
        for k, p in enumerate(peers)
    ]
    out_in[plane, place] = out_own[c]
    for copy in outs:
        copy.wait_recv()
    out_ref[...] = out_in[...]
    for copy in pending:
        copy.wait_send()


def band_body(gx_n, gy_n, estimate, views, psf_rows, psf_cols, shifts, codes):
    views_n, depth, tile_rows, width = views.shape
    blocks_n = shifts.shape[1]
    block_rows = tile_rows // blocks_n
    part_n = blocks_n // 2
    part_rows = part_n * block_rows
    near_rows = part_rows + 2 * NEAR * block_rows
    band_rows = part_rows + 2 * HALO * block_rows
    others = gy_n - 1
    vmem = pltpu.VMEM
    dma = pltpu.SemaphoreType.DMA
    out = pl.pallas_call(
        functools.partial(kernel, gx_n, gy_n),
        out_shape=pltpu.VMEM((depth, blocks_n, block_rows, width), F32),
        in_specs=[pl.BlockSpec(memory_space=pltpu.HBM)] * 6,
        out_specs=pl.BlockSpec(memory_space=pltpu.VMEM),
        scratch_shapes=[
            vmem((depth, blocks_n, block_rows, width), F32),
            vmem(views.shape, BF16),
            vmem(shifts.shape, jnp.int32),
            vmem((views_n, blocks_n), jnp.int32),
            pltpu.SMEM(psf_rows.shape, F32),
            pltpu.SMEM(psf_cols.shape, F32),
            vmem((width, width), F32),
            vmem((2, 8, width), F32),
            vmem((ITERS, gy_n, part_n + 2 * HALO, block_rows, width), F32),
            vmem((views_n, depth, blocks_n, block_rows, width), F32),
            vmem((views_n, gy_n, part_n + 2 * NEAR, block_rows, width), F32),
            vmem((gy_n, 4, 8, width), F32),
            vmem((views_n, gy_n + 1, 4 * 8, width), F32),
            vmem((views_n, gy_n, part_n + 2 * HALO, block_rows, width), F32),
            vmem((views_n, part_n + 2 * HALO, block_rows, width), F32),
            vmem((gy_n, part_n, block_rows, width), F32),
            vmem((depth, blocks_n, block_rows, width), F32),
            vmem((views_n, near_rows, 3 * band_rows), BF16),
            vmem((views_n, part_rows, 3 * near_rows), BF16),
            vmem((views_n, 6 * width, 2 * width), BF16),
            vmem((views_n, 6 * width, 2 * width), BF16),
            dma((6,)),
            dma((others,)), dma((others,)),
            dma((2 * ITERS - 1,)), dma((2 * ITERS - 1,)),
            dma((views_n, others)), dma((views_n, others)),
            dma((views_n, 2)), dma((views_n, 2)),
            dma((others,)), dma((others,)),
            dma((1,)), dma((1,)),
            dma((others,)), dma((others,)),
        ],
        compiler_params=pltpu.CompilerParams(
            collective_id=0, has_side_effects=True, vmem_limit_bytes=56 * 1024 * 1024
        ),
    )(
        estimate.reshape(depth, blocks_n, block_rows, width), views, shifts,
        codes.reshape(views_n, blocks_n), psf_rows, psf_cols,
    )
    return out.reshape(depth, tile_rows, width)


def solution(mesh):
    placed = (
        P(None, "gx", "gy"),
        P(None, None, "gx", "gy"),
        P(),
        P(),
        P(None, "gx"),
        P(None, "gx", "gy"),
    )
    gx_n, gy_n = mesh.shape["gx"], mesh.shape["gy"]

    def body(estimate, views, *rest):
        parts_n = 2 * estimate.shape[0]
        if gy_n == parts_n and gx_n % 2 == 0 and rest[2].shape[1] == 16:
            return band_body(gx_n, gy_n, estimate, views, *rest)
        return tile_body(estimate, views, *rest)

    return jax.shard_map(
        body, mesh=mesh, in_specs=placed, out_specs=P(None, "gx", "gy"), check_vma=False
    )
```

```python
import functools

import jax
import jax.numpy as jnp
from jax import lax
from jax.experimental import pallas as pl
from jax.experimental.pallas import tpu as pltpu
from jax.sharding import PartitionSpec as P

ITERS = 2
MESH = pl.DeviceIdType.MESH
F32 = jnp.float32
BF16 = jnp.bfloat16
HALO = 4
NEAR = 2


def with_halo(block, sides, width):
    for axis, dim in sides:
        count = lax.axis_size(axis)
        forward = [(i, i + 1) for i in range(count - 1)]
        backward = [(target, source) for source, target in forward]
        low = lax.ppermute(
            lax.slice_in_dim(block, block.shape[dim] - width, None, axis=dim), axis, forward
        )
        high = lax.ppermute(lax.slice_in_dim(block, 0, width, axis=dim), axis, backward)
        block = jnp.concatenate([low, block, high], axis=dim)
    return block


def shift_in(values, fraction):
    last = values.shape[-1] - 1
    column = lax.broadcasted_iota(jnp.int32, values.shape, values.ndim - 1)
    following = jnp.concatenate([values[..., 1:], values[..., -1:]], axis=-1)
    return jnp.where(column < last, (1.0 - fraction) * values + fraction * following, values)


def shift_back(values, fraction):
    last = values.shape[-1] - 1
    column = lax.broadcasted_iota(jnp.int32, values.shape, values.ndim - 1)
    preceding = jnp.concatenate([jnp.zeros_like(values[..., :1]), values[..., :-1]], axis=-1)
    own_part = jnp.where(column < last, (1.0 - fraction) * values, values)
    return own_part + fraction * preceding


def smooth_rows(padded, taps, count):
    total = taps[0] * padded[..., 0:count, :]
    for offset in range(1, taps.shape[0]):
        total = total + taps[offset] * padded[..., offset : offset + count, :]
    return total


def smooth_cols(padded, taps, count):
    total = taps[0] * padded[..., 0:count]
    for offset in range(1, taps.shape[0]):
        total = total + taps[offset] * padded[..., offset : offset + count]
    return total


def tile_body(estimate, views, psf_rows, psf_cols, shifts, codes):
    highest = lax.Precision.HIGHEST
    groups = lax.axis_size("gy")
    column = lax.axis_index("gy")
    views_n, depth, tile_rows, tile_cols = views.shape
    blocks_n = shifts.shape[1]
    block_rows = tile_rows // blocks_n
    capacity = 1 + (blocks_n + groups - 2) // groups
    tap_count = psf_rows.shape[1]
    half = tap_count // 2
    kern_rows = psf_rows / jnp.sum(psf_rows, axis=1, keepdims=True)
    kern_cols = psf_cols / jnp.sum(psf_cols, axis=1, keepdims=True)
    taps_rows = kern_rows.T.reshape(tap_count, views_n, 1, 1, 1)
    taps_cols = kern_cols.T.reshape(tap_count, views_n, 1, 1, 1)
    flipped_rows = kern_rows[:, ::-1].T.reshape(tap_count, views_n, 1, 1, 1)
    flipped_cols = kern_cols[:, ::-1].T.reshape(tap_count, views_n, 1, 1, 1)
    fraction = (codes[:, :, 0].astype(jnp.float32) / 16.0)[:, None, :, None, None]
    block_ids = jnp.arange(blocks_n, dtype=jnp.int32)
    same_shift = shifts[:, :, None] == shifts[:, None, :]
    earlier = block_ids[None, None, :] < block_ids[None, :, None]
    slot_rank = jnp.sum((same_shift & earlier).astype(jnp.int32), axis=2)
    peer_ids = jnp.arange(groups, dtype=jnp.int32)
    slot_ids = jnp.arange(capacity, dtype=jnp.int32)
    source_peer = (column + shifts) % groups
    target_peer = (column - shifts) % groups
    send_hot = (
        (peer_ids[None, :, None, None] == target_peer[:, None, None, :])
        & (slot_ids[None, None, :, None] == slot_rank[:, None, None, :])
    ).astype(jnp.float32)
    recv_hot = (
        (peer_ids[None, None, :, None] == source_peer[:, :, None, None])
        & (slot_ids[None, None, None, :] == slot_rank[:, :, None, None])
    ).astype(jnp.float32)
    for sweep in range(ITERS):
        blocked = estimate.reshape(depth, blocks_n, block_rows, tile_cols)
        outgoing = jnp.einsum("vpqk,zkrw->pvqzrw", send_hot, blocked, precision=highest)
        arriving = lax.all_to_all(outgoing, "gy", split_axis=0, concat_axis=0, tiled=True)
        view_blocks = jnp.einsum("vkpq,pvqzrw->vzkrw", recv_hot, arriving, precision=highest)
        view_est = shift_in(view_blocks, fraction).reshape(views_n, depth, tile_rows, tile_cols)
        padded = with_halo(view_est, (("gx", 2), ("gy", 3)), half)
        rows_done = smooth_rows(padded, taps_rows, tile_rows)
        blurred = smooth_cols(rows_done, taps_cols, tile_cols)
        ratio = views.astype(jnp.float32) / blurred
        padded_ratio = with_halo(ratio, (("gx", 2), ("gy", 3)), half)
        rows_back = smooth_rows(padded_ratio, flipped_rows, tile_rows)
        back = smooth_cols(rows_back, flipped_cols, tile_cols)
        returned = shift_back(
            back.reshape(views_n, depth, blocks_n, block_rows, tile_cols), fraction
        )
        leaving = jnp.einsum("vkpq,vzkrw->pvqzrw", recv_hot, returned, precision=highest)
        coming = lax.all_to_all(leaving, "gy", split_axis=0, concat_axis=0, tiled=True)
        summed = jnp.einsum("vpqk,pvqzrw->zkrw", send_hot, coming, precision=highest)
        estimate = estimate * (summed.reshape(depth, tile_rows, tile_cols) / views_n)
    return estimate


def split(value):
    high = value.astype(BF16)
    return high, (value - high.astype(F32)).astype(BF16)


def store_terms(ref, rows, cols, step, value):
    high, low = split(value)
    for k, part in enumerate((high, high, low)):
        ref[pl.ds(rows + k * step, value.shape[0]), pl.ds(cols, value.shape[1])] = part


def terms(value):
    high, low = split(value)
    return jnp.concatenate([high, low, high], axis=1)


def product(left, right):
    return lax.dot_general(left, right, (((1,), (0,)), ((), ())), preferred_element_type=F32)


def store_halves(ref, value):
    rows, cols = value.shape
    for k, part in enumerate(split(value)):
        for j in range(2):
            ref[pl.ds(k * rows, rows), pl.ds(j * cols, cols)] = part


def rows_by(band, field):
    done = product(band[...], jnp.concatenate(split(field), axis=0))
    rows = done.shape[0] // 2
    return done[:rows] + done[rows:]


def cols_by(field, band):
    width = band.shape[1] // 2
    rows = field.shape[0]
    count = field.shape[1] // width - 1
    windows = [field[:, j * width : (j + 2) * width] for j in range(count)]
    done = product(terms(jnp.concatenate(windows, axis=0)), band[...])
    done = [done[j * rows : (j + 1) * rows] for j in range(count)]
    lane = lax.broadcasted_iota(jnp.int32, (rows, width), 1)
    tiles = [done[0][:, :width]]
    for j in range(count - 1):
        tiles.append(jnp.where(lane < width // 2, done[j][:, width:], done[j + 1][:, :width]))
    tiles.append(done[-1][:, width:])
    return tiles


def taps_of(ref, view):
    taps = [ref[view, t] for t in range(ref.shape[1])]
    return taps, functools.reduce(lambda a, b: a + b, taps)


def banded(taps, total, offset):
    value = jnp.zeros(offset.shape, F32)
    for t, tap in enumerate(taps):
        value = jnp.where(offset == t, tap, value)
    return value / jnp.full(offset.shape, total, F32)


def kernel(
    gx_n, gy_n, est_hbm, views_hbm, shifts_hbm, codes_hbm, psf_rows_hbm, psf_cols_hbm, out_ref,
    est_ref, views_ref, shifts_ref, codes_ref, psf_rows_ref, psf_cols_ref, meta_wide, meta_ref,
    est_band, views_out, views_band, meta_band, lines, frac_full, shift_full, out_own, out_in,
    band_fwd, band_back, cols_fwd, cols_back,
    local, gather_s, gather_r, halo_s, halo_r, views_s, views_r, near_s, near_r,
    meta_s, meta_r, edge_s, edge_r, out_s, out_r,
):
    views_n, depth, _, width = views_ref.shape
    blocks_n, block_rows = est_ref.shape[1:3]
    part_n = blocks_n // 2
    part_rows = part_n * block_rows
    band_rows = (part_n + 2 * HALO) * block_rows
    near_rows = (part_n + 2 * NEAR) * block_rows
    half = psf_rows_ref.shape[1] // 2
    g = lax.axis_index("gx")
    c = lax.axis_index("gy")

    def place_of(device):
        return device // 2, lax.rem(device + g, 2)

    plane, h = place_of(c)
    peers = [lax.rem(c + k, gy_n) for k in range(1, gy_n)]
    partner = {"gy": c + 1 - 2 * lax.rem(c, 2)}
    beside = {"gx": lax.rem(g - 1 + 2 * h + gx_n, gx_n)}
    pending = []

    def send(src, dst, send_sem, recv_sem, target):
        copy = pltpu.make_async_remote_copy(
            src_ref=src, dst_ref=dst, send_sem=send_sem, recv_sem=recv_sem,
            device_id=target, device_id_type=MESH,
        )
        copy.start()
        pending.append(copy)
        return copy

    loads = [
        pltpu.make_async_copy(src, dst, local.at[k])
        for k, (src, dst) in enumerate(
            (
                (codes_hbm, codes_ref), (shifts_hbm, shifts_ref), (est_hbm, est_ref),
                (views_hbm, views_ref), (psf_rows_hbm, psf_rows_ref), (psf_cols_hbm, psf_cols_ref),
            )
        )
    ]
    for load in loads:
        load.start()
    barrier = pltpu.get_barrier_semaphore()
    for target in [{"gy": p} for p in peers] + [beside]:
        pl.semaphore_signal(barrier, inc=1, device_id=target, device_id_type=MESH)
    meta_wide[...] = jnp.zeros(meta_wide.shape, F32)
    for load in loads[:2]:
        load.wait()
    meta_wide[pl.ds(0, views_n), pl.ds(0, blocks_n)] = codes_ref[...].astype(F32) / 16.0
    meta_wide[pl.ds(views_n, views_n), pl.ds(0, blocks_n)] = shifts_ref[...].astype(F32)
    meta_ref[...] = meta_wide[...].T[:blocks_n].reshape(meta_ref.shape)
    loads[2].wait()
    pl.semaphore_wait(barrier, gy_n)

    meta_copies = [
        send(meta_ref, meta_band.at[c, pl.ds(1, 2)], meta_s.at[k], meta_r.at[k], {"gy": p})
        for k, p in enumerate(peers)
    ]
    est_n = part_n + HALO
    gathers = []
    for k, p in enumerate(peers):
        layer, other = place_of(p)
        gathers.append(
            send(
                est_ref.at[layer, pl.ds(HALO * other, est_n)],
                est_band.at[0, c, pl.ds(HALO - HALO * other, est_n)],
                gather_s.at[k], gather_r.at[k], {"gy": p},
            )
        )
    loads[3].wait()
    for view in range(views_n):
        for layer in range(depth):
            views_out[view, layer] = (
                views_ref[view, layer].astype(F32).reshape(blocks_n, block_rows, width)
            )
    seen = pl.ds(NEAR, part_n)
    view_copies = []

    def send_view(view):
        copies = []
        for k, p in enumerate(peers):
            layer, other = place_of(p)
            copies.append(
                send(
                    views_out.at[view, layer, pl.ds(part_n * other, part_n)],
                    views_band.at[view, c, seen],
                    views_s.at[view, k], views_r.at[view, k], {"gy": p},
                )
            )
        view_copies.append(copies)

    send_view(0)
    meta_band[c, pl.ds(1, 2)] = meta_ref[...]
    est_band[0, c, pl.ds(HALO - HALO * h, est_n)] = est_ref[plane, pl.ds(HALO * h, est_n)]
    for view in range(views_n):
        views_band[view, c, seen] = views_out[view, plane, pl.ds(part_n * h, part_n)]

    for load in loads[4:]:
        load.wait()
    first_row = jnp.where((g == 0) & (h == 0), 0, -HALO * block_rows)
    last_row = jnp.where((g == gx_n - 1) & (h == 1), part_rows, part_rows + HALO * block_rows)
    for view in range(views_n):
        taps, total = taps_of(psf_rows_ref, view)
        row = lax.broadcasted_iota(jnp.int32, (near_rows, band_rows), 0) - NEAR * block_rows
        col = lax.broadcasted_iota(jnp.int32, (near_rows, band_rows), 1) - HALO * block_rows
        inside = (col >= first_row) & (col < last_row)
        outer = (row < first_row) | (row >= last_row)
        value = jnp.where(inside | outer, banded(taps, total, col - row + half), 0.0)
        store_halves(band_fwd.at[view], value)
        row = lax.broadcasted_iota(jnp.int32, (part_rows, near_rows), 0)
        col = lax.broadcasted_iota(jnp.int32, (part_rows, near_rows), 1) - NEAR * block_rows
        inside = (col >= first_row) & (col < last_row)
        value = jnp.where(inside, banded(taps, total, row - col + half), 0.0)
        store_halves(band_back.at[view], value)
        taps, total = taps_of(psf_cols_ref, view)
        for ref, sign in ((cols_fwd.at[view], 1), (cols_back.at[view], -1)):
            row = lax.broadcasted_iota(jnp.int32, (width, width), 0)
            col = lax.broadcasted_iota(jnp.int32, (width, width), 1)
            value = banded(taps, total, sign * (row - col) + half)
            store_terms(ref, 0, 0, 2 * width, value)
            store_terms(ref, width, width, 2 * width, value)
            row, col = row[:16], col[:16]
            blank = jnp.zeros((width - 16, width), F32)
            value = banded(taps, total, sign * (row + width - col) + half)
            value = jnp.concatenate([value, blank], axis=0)
            store_terms(ref, width, 0, 2 * width, value)
            value = banded(taps, total, sign * (row - 16 - col) + half)
            value = jnp.concatenate([blank, value], axis=0)
            store_terms(ref, 0, width, 2 * width, value)

    for copy in meta_copies:
        copy.wait_recv()
    edge = send(
        meta_band.at[:, 1 + h], meta_band.at[:, 3 - 3 * h], edge_s.at[0], edge_r.at[0], beside
    )
    for copy in gathers:
        copy.wait_recv()
    halo = send(
        est_band.at[0, :, pl.ds(HALO + (part_n - HALO) * h, HALO)],
        est_band.at[0, :, pl.ds((part_n + HALO) * (1 - h), HALO)],
        halo_s.at[0], halo_r.at[0], beside,
    )
    send_view(1)
    send_view(2)

    edge.wait_recv()
    for j in range(gy_n):
        found = meta_band[j].reshape(4 * 8, width)
        for view in range(views_n):
            lines[view, j] = jnp.broadcast_to(found[:, view : view + 1], found.shape)
            if j == 0:
                near = found[:, views_n + view : views_n + view + 1]
                lines[view, gy_n] = jnp.broadcast_to(near, found.shape)

    lane = lax.broadcasted_iota(jnp.int32, (block_rows, width), 1)

    def spread(b, carry):
        place = pl.ds(b + 8 - HALO + part_n * h, 1)
        for view in range(views_n):
            for j in range(gy_n):
                line = jnp.broadcast_to(lines[view, j, place, :], (block_rows, width))
                frac_full[view, j, b] = jnp.where(lane < width - 1, line, 0.0)
            shift_full[view, b] = jnp.broadcast_to(
                lines[view, gy_n, place, :], (block_rows, width)
            )
        return carry

    lax.fori_loop(0, part_n + 2 * HALO, spread, 0)
    halo.wait_recv()

    def pick(shift, tiles, first, sign):
        value = tiles[first % gy_n]
        for k in range(1, gy_n):
            value = jnp.where(shift == float(k), tiles[(first + sign * k) % gy_n], value)
        return value

    own = pl.ds(HALO, part_n)

    def viewed(sweep, view, start, count):
        place = pl.ds(start, count)
        rows = count * block_rows
        shift = shift_full[view, place]
        tiles = [est_band[sweep, j, place] for j in range(gy_n)]
        parts = []
        for j in range(gy_n):
            moved = pick(shift, tiles, j, 1).reshape(rows, width)
            fraction = frac_full[view, j, place].reshape(rows, width)
            following = pltpu.roll(moved, width - 1, 1)
            parts.append(moved + fraction * (following - moved))
        return jnp.concatenate(parts, axis=1)

    def blur(sweep, views):
        fields = [viewed(sweep, view, 0, part_n + 2 * HALO) for view in views]
        fields = [rows_by(band_fwd.at[view], x) for view, x in zip(views, fields)]
        return [cols_by(x, cols_fwd.at[view]) for view, x in zip(views, fields)]

    def blur_cols_first(sweep, views, halos):
        inner = [viewed(sweep, view, HALO, part_n) for view in views]
        inner = [cols_by(x, cols_fwd.at[view]) for view, x in zip(views, inner)]
        inner = [jnp.concatenate(tiles, axis=1) for tiles in inner]
        for copy in halos:
            copy.wait_recv()
        cut = HALO * block_rows
        outer = [
            jnp.concatenate(
                [viewed(sweep, view, 0, HALO), viewed(sweep, view, HALO + part_n, HALO)], axis=0
            )
            for view in views
        ]
        outer = [cols_by(x, cols_fwd.at[view]) for view, x in zip(views, outer)]
        outer = [jnp.concatenate(tiles, axis=1) for tiles in outer]
        fields = [jnp.concatenate([o[:cut], i, o[cut:]], axis=0) for i, o in zip(inner, outer)]
        fields = [rows_by(band_fwd.at[view], x) for view, x in zip(views, fields)]
        return [[x[:, j * width : (j + 1) * width] for j in range(gy_n)] for x in fields]

    def correct(views, blurred):
        ratio = [
            [views_band[view, j].reshape(near_rows, width) / tiles[j] for j in range(gy_n)]
            for view, tiles in zip(views, blurred)
        ]
        fields = [
            rows_by(band_back.at[view], jnp.concatenate(tiles, axis=1))
            for view, tiles in zip(views, ratio)
        ]
        back = [cols_by(x, cols_back.at[view]) for view, x in zip(views, fields)]
        homes = []
        for view, tiles in zip(views, back):
            returned = []
            for j in range(gy_n):
                passed = frac_full[view, j, own].reshape(part_rows, width) * tiles[j]
                value = tiles[j] - passed + pltpu.roll(passed, 1, 1)
                returned.append(value.reshape(part_n, block_rows, width))
            shift = shift_full[view, own]
            homes.append([pick(shift, returned, j, -1) for j in range(gy_n)])
        return homes

    def add_up(all_homes):
        return functools.reduce(lambda x, y: [a + b for a, b in zip(x, y)], all_homes)

    def arrive(view):
        for copy in view_copies[view]:
            copy.wait_recv()
        band = views_band.at[view]
        nears = [
            send(
                band.at[:, pl.ds(part_n - (part_n - NEAR) * h, NEAR)],
                band.at[:, pl.ds((part_n + NEAR) * h, NEAR)],
                near_s.at[view, 0], near_r.at[view, 0], partner,
            ),
            send(
                band.at[:, pl.ds(NEAR + (part_n - NEAR) * h, NEAR)],
                band.at[:, pl.ds((part_n + NEAR) * (1 - h), NEAR)],
                near_s.at[view, 1], near_r.at[view, 1], beside,
            ),
        ]
        if view + 3 < views_n:
            send_view(view + 3)
        return nears

    for sweep in range(ITERS):
        if sweep == 0:
            nears = []
            blurred = []
            for view in range(0, views_n, 2):
                blurred += blur(sweep, list(range(view, min(view + 2, views_n))))
                nears.append(arrive(view // 2))
            homes = []
            for view in range(views_n):
                if len(nears) < min(view + 2, views_n):
                    nears.append(arrive(len(nears)))
                for copy in nears[view]:
                    copy.wait_recv()
                homes += correct([view], [blurred[view]])
        else:
            every = list(range(views_n))
            homes = correct(every, blur_cols_first(sweep, every, halos))
        sums = add_up(homes)
        updated = [est_band[sweep, j, own] * (sums[j] / views_n) for j in range(gy_n)]
        if sweep + 1 < ITERS:
            for j in range(gy_n):
                est_band[sweep + 1, j, own] = updated[j]
            band = est_band.at[sweep + 1]
            halos = [
                send(
                    band.at[:, pl.ds(part_n - (part_n - HALO) * h, HALO)],
                    band.at[:, pl.ds((part_n + HALO) * h, HALO)],
                    halo_s.at[2 * sweep + 1], halo_r.at[2 * sweep + 1], partner,
                ),
                send(
                    band.at[:, pl.ds(HALO + (part_n - HALO) * h, HALO)],
                    band.at[:, pl.ds((part_n + HALO) * (1 - h), HALO)],
                    halo_s.at[2 * sweep + 2], halo_r.at[2 * sweep + 2], beside,
                ),
            ]
    for j in range(gy_n):
        out_own[j] = updated[j]
    place = pl.ds(part_n * h, part_n)
    outs = [
        send(out_own.at[p], out_in.at[plane, place], out_s.at[k], out_r.at[k], {"gy": p})
        for k, p in enumerate(peers)
    ]
    out_in[plane, place] = out_own[c]
    for copy in outs:
        copy.wait_recv()
    out_ref[...] = out_in[...]
    for copy in pending:
        copy.wait_send()


def band_body(gx_n, gy_n, estimate, views, psf_rows, psf_cols, shifts, codes):
    views_n, depth, tile_rows, width = views.shape
    blocks_n = shifts.shape[1]
    block_rows = tile_rows // blocks_n
    part_n = blocks_n // 2
    part_rows = part_n * block_rows
    near_rows = part_rows + 2 * NEAR * block_rows
    band_rows = part_rows + 2 * HALO * block_rows
    others = gy_n - 1
    vmem = pltpu.VMEM
    dma = pltpu.SemaphoreType.DMA
    out = pl.pallas_call(
        functools.partial(kernel, gx_n, gy_n),
        out_shape=pltpu.VMEM((depth, blocks_n, block_rows, width), F32),
        in_specs=[pl.BlockSpec(memory_space=pltpu.HBM)] * 6,
        out_specs=pl.BlockSpec(memory_space=pltpu.VMEM),
        scratch_shapes=[
            vmem((depth, blocks_n, block_rows, width), F32),
            vmem(views.shape, BF16),
            vmem(shifts.shape, jnp.int32),
            vmem((views_n, blocks_n), jnp.int32),
            pltpu.SMEM(psf_rows.shape, F32),
            pltpu.SMEM(psf_cols.shape, F32),
            vmem((width, width), F32),
            vmem((2, 8, width), F32),
            vmem((ITERS, gy_n, part_n + 2 * HALO, block_rows, width), F32),
            vmem((views_n, depth, blocks_n, block_rows, width), F32),
            vmem((views_n, gy_n, part_n + 2 * NEAR, block_rows, width), F32),
            vmem((gy_n, 4, 8, width), F32),
            vmem((views_n, gy_n + 1, 4 * 8, width), F32),
            vmem((views_n, gy_n, part_n + 2 * HALO, block_rows, width), F32),
            vmem((views_n, part_n + 2 * HALO, block_rows, width), F32),
            vmem((gy_n, part_n, block_rows, width), F32),
            vmem((depth, blocks_n, block_rows, width), F32),
            vmem((views_n, 2 * near_rows, 2 * band_rows), BF16),
            vmem((views_n, 2 * part_rows, 2 * near_rows), BF16),
            vmem((views_n, 6 * width, 2 * width), BF16),
            vmem((views_n, 6 * width, 2 * width), BF16),
            dma((6,)),
            dma((others,)), dma((others,)),
            dma((2 * ITERS - 1,)), dma((2 * ITERS - 1,)),
            dma((views_n, others)), dma((views_n, others)),
            dma((views_n, 2)), dma((views_n, 2)),
            dma((others,)), dma((others,)),
            dma((1,)), dma((1,)),
            dma((others,)), dma((others,)),
        ],
        compiler_params=pltpu.CompilerParams(
            collective_id=0, has_side_effects=True, vmem_limit_bytes=56 * 1024 * 1024
        ),
    )(
        estimate.reshape(depth, blocks_n, block_rows, width), views, shifts,
        codes.reshape(views_n, blocks_n), psf_rows, psf_cols,
    )
    return out.reshape(depth, tile_rows, width)


def solution(mesh):
    placed = (
        P(None, "gx", "gy"),
        P(None, None, "gx", "gy"),
        P(),
        P(),
        P(None, "gx"),
        P(None, "gx", "gy"),
    )
    gx_n, gy_n = mesh.shape["gx"], mesh.shape["gy"]

    def body(estimate, views, *rest):
        parts_n = 2 * estimate.shape[0]
        if gy_n == parts_n and gx_n % 2 == 0 and rest[2].shape[1] == 16:
            return band_body(gx_n, gy_n, estimate, views, *rest)
        return tile_body(estimate, views, *rest)

    return jax.shard_map(
        body, mesh=mesh, in_specs=placed, out_specs=P(None, "gx", "gy"), check_vma=False
    )
```

```python
import functools

import jax
import jax.numpy as jnp
from jax import lax
from jax.experimental import pallas as pl
from jax.experimental.pallas import tpu as pltpu
from jax.sharding import PartitionSpec as P

ITERS = 2
MESH = pl.DeviceIdType.MESH
F32 = jnp.float32
BF16 = jnp.bfloat16
HALO = 4
NEAR = 2


def with_halo(block, sides, width):
    for axis, dim in sides:
        count = lax.axis_size(axis)
        forward = [(i, i + 1) for i in range(count - 1)]
        backward = [(target, source) for source, target in forward]
        low = lax.ppermute(
            lax.slice_in_dim(block, block.shape[dim] - width, None, axis=dim), axis, forward
        )
        high = lax.ppermute(lax.slice_in_dim(block, 0, width, axis=dim), axis, backward)
        block = jnp.concatenate([low, block, high], axis=dim)
    return block


def shift_in(values, fraction):
    last = values.shape[-1] - 1
    column = lax.broadcasted_iota(jnp.int32, values.shape, values.ndim - 1)
    following = jnp.concatenate([values[..., 1:], values[..., -1:]], axis=-1)
    return jnp.where(column < last, (1.0 - fraction) * values + fraction * following, values)


def shift_back(values, fraction):
    last = values.shape[-1] - 1
    column = lax.broadcasted_iota(jnp.int32, values.shape, values.ndim - 1)
    preceding = jnp.concatenate([jnp.zeros_like(values[..., :1]), values[..., :-1]], axis=-1)
    own_part = jnp.where(column < last, (1.0 - fraction) * values, values)
    return own_part + fraction * preceding


def smooth_rows(padded, taps, count):
    total = taps[0] * padded[..., 0:count, :]
    for offset in range(1, taps.shape[0]):
        total = total + taps[offset] * padded[..., offset : offset + count, :]
    return total


def smooth_cols(padded, taps, count):
    total = taps[0] * padded[..., 0:count]
    for offset in range(1, taps.shape[0]):
        total = total + taps[offset] * padded[..., offset : offset + count]
    return total


def tile_body(estimate, views, psf_rows, psf_cols, shifts, codes):
    highest = lax.Precision.HIGHEST
    groups = lax.axis_size("gy")
    column = lax.axis_index("gy")
    views_n, depth, tile_rows, tile_cols = views.shape
    blocks_n = shifts.shape[1]
    block_rows = tile_rows // blocks_n
    capacity = 1 + (blocks_n + groups - 2) // groups
    tap_count = psf_rows.shape[1]
    half = tap_count // 2
    kern_rows = psf_rows / jnp.sum(psf_rows, axis=1, keepdims=True)
    kern_cols = psf_cols / jnp.sum(psf_cols, axis=1, keepdims=True)
    taps_rows = kern_rows.T.reshape(tap_count, views_n, 1, 1, 1)
    taps_cols = kern_cols.T.reshape(tap_count, views_n, 1, 1, 1)
    flipped_rows = kern_rows[:, ::-1].T.reshape(tap_count, views_n, 1, 1, 1)
    flipped_cols = kern_cols[:, ::-1].T.reshape(tap_count, views_n, 1, 1, 1)
    fraction = (codes[:, :, 0].astype(jnp.float32) / 16.0)[:, None, :, None, None]
    block_ids = jnp.arange(blocks_n, dtype=jnp.int32)
    same_shift = shifts[:, :, None] == shifts[:, None, :]
    earlier = block_ids[None, None, :] < block_ids[None, :, None]
    slot_rank = jnp.sum((same_shift & earlier).astype(jnp.int32), axis=2)
    peer_ids = jnp.arange(groups, dtype=jnp.int32)
    slot_ids = jnp.arange(capacity, dtype=jnp.int32)
    source_peer = (column + shifts) % groups
    target_peer = (column - shifts) % groups
    send_hot = (
        (peer_ids[None, :, None, None] == target_peer[:, None, None, :])
        & (slot_ids[None, None, :, None] == slot_rank[:, None, None, :])
    ).astype(jnp.float32)
    recv_hot = (
        (peer_ids[None, None, :, None] == source_peer[:, :, None, None])
        & (slot_ids[None, None, None, :] == slot_rank[:, :, None, None])
    ).astype(jnp.float32)
    for sweep in range(ITERS):
        blocked = estimate.reshape(depth, blocks_n, block_rows, tile_cols)
        outgoing = jnp.einsum("vpqk,zkrw->pvqzrw", send_hot, blocked, precision=highest)
        arriving = lax.all_to_all(outgoing, "gy", split_axis=0, concat_axis=0, tiled=True)
        view_blocks = jnp.einsum("vkpq,pvqzrw->vzkrw", recv_hot, arriving, precision=highest)
        view_est = shift_in(view_blocks, fraction).reshape(views_n, depth, tile_rows, tile_cols)
        padded = with_halo(view_est, (("gx", 2), ("gy", 3)), half)
        rows_done = smooth_rows(padded, taps_rows, tile_rows)
        blurred = smooth_cols(rows_done, taps_cols, tile_cols)
        ratio = views.astype(jnp.float32) / blurred
        padded_ratio = with_halo(ratio, (("gx", 2), ("gy", 3)), half)
        rows_back = smooth_rows(padded_ratio, flipped_rows, tile_rows)
        back = smooth_cols(rows_back, flipped_cols, tile_cols)
        returned = shift_back(
            back.reshape(views_n, depth, blocks_n, block_rows, tile_cols), fraction
        )
        leaving = jnp.einsum("vkpq,vzkrw->pvqzrw", recv_hot, returned, precision=highest)
        coming = lax.all_to_all(leaving, "gy", split_axis=0, concat_axis=0, tiled=True)
        summed = jnp.einsum("vpqk,pvqzrw->zkrw", send_hot, coming, precision=highest)
        estimate = estimate * (summed.reshape(depth, tile_rows, tile_cols) / views_n)
    return estimate


def split(value):
    high = value.astype(BF16)
    return high, (value - high.astype(F32)).astype(BF16)


def store_terms(ref, rows, cols, step, value):
    high, low = split(value)
    for k, part in enumerate((high, high, low)):
        ref[pl.ds(rows + k * step, value.shape[0]), pl.ds(cols, value.shape[1])] = part


def terms(value):
    high, low = split(value)
    return jnp.concatenate([high, low, high], axis=1)


def product(left, right):
    return lax.dot_general(left, right, (((1,), (0,)), ((), ())), preferred_element_type=F32)


def store_halves(ref, value):
    rows, cols = value.shape
    for k, part in enumerate(split(value)):
        for j in range(2):
            ref[pl.ds(k * rows, rows), pl.ds(j * cols, cols)] = part


def rows_by(band, field):
    done = product(band[...], jnp.concatenate(split(field), axis=0))
    rows = done.shape[0] // 2
    return done[:rows] + done[rows:]


def cols_by(field, band):
    width = band.shape[1] // 2
    rows = field.shape[0]
    count = field.shape[1] // width - 1
    windows = [field[:, j * width : (j + 2) * width] for j in range(count)]
    done = product(terms(jnp.concatenate(windows, axis=0)), band[...])
    done = [done[j * rows : (j + 1) * rows] for j in range(count)]
    lane = lax.broadcasted_iota(jnp.int32, (rows, width), 1)
    tiles = [done[0][:, :width]]
    for j in range(count - 1):
        tiles.append(jnp.where(lane < width // 2, done[j][:, width:], done[j + 1][:, :width]))
    tiles.append(done[-1][:, width:])
    return tiles


def taps_of(ref, view):
    taps = [ref[view, t] for t in range(ref.shape[1])]
    return taps, functools.reduce(lambda a, b: a + b, taps)


def banded(taps, total, offset):
    value = jnp.zeros(offset.shape, F32)
    for t, tap in enumerate(taps):
        value = jnp.where(offset == t, tap, value)
    return value / jnp.full(offset.shape, total, F32)


def kernel(
    gx_n, gy_n, est_hbm, views_hbm, shifts_hbm, codes_hbm, psf_rows_hbm, psf_cols_hbm, out_ref,
    est_ref, views_ref, shifts_ref, codes_ref, psf_rows_ref, psf_cols_ref, meta_wide, meta_ref,
    est_band, views_out, views_band, meta_band, lines, frac_full, shift_full, out_own, out_in,
    band_fwd, band_back, cols_fwd, cols_back,
    local, gather_s, gather_r, halo_s, halo_r, views_s, views_r, near_s, near_r,
    meta_s, meta_r, edge_s, edge_r, out_s, out_r,
):
    views_n, depth, _, width = views_ref.shape
    blocks_n, block_rows = est_ref.shape[1:3]
    part_n = blocks_n // 2
    part_rows = part_n * block_rows
    band_rows = (part_n + 2 * HALO) * block_rows
    near_rows = (part_n + 2 * NEAR) * block_rows
    half = psf_rows_ref.shape[1] // 2
    g = lax.axis_index("gx")
    c = lax.axis_index("gy")

    def place_of(device):
        return device // 2, lax.rem(device + g, 2)

    plane, h = place_of(c)
    peers = [lax.rem(c + k, gy_n) for k in range(1, gy_n)]
    partner = {"gy": c + 1 - 2 * lax.rem(c, 2)}
    beside = {"gx": lax.rem(g - 1 + 2 * h + gx_n, gx_n)}
    pending = []

    def send(src, dst, send_sem, recv_sem, target):
        copy = pltpu.make_async_remote_copy(
            src_ref=src, dst_ref=dst, send_sem=send_sem, recv_sem=recv_sem,
            device_id=target, device_id_type=MESH,
        )
        copy.start()
        pending.append(copy)
        return copy

    loads = [
        pltpu.make_async_copy(src, dst, local.at[k])
        for k, (src, dst) in enumerate(
            (
                (codes_hbm, codes_ref), (shifts_hbm, shifts_ref), (est_hbm, est_ref),
                (views_hbm, views_ref), (psf_rows_hbm, psf_rows_ref), (psf_cols_hbm, psf_cols_ref),
            )
        )
    ]
    for load in loads:
        load.start()
    barrier = pltpu.get_barrier_semaphore()
    for target in [{"gy": p} for p in peers] + [beside]:
        pl.semaphore_signal(barrier, inc=1, device_id=target, device_id_type=MESH)
    meta_wide[...] = jnp.zeros(meta_wide.shape, F32)
    for load in loads[:2]:
        load.wait()
    meta_wide[pl.ds(0, views_n), pl.ds(0, blocks_n)] = codes_ref[...].astype(F32) / 16.0
    meta_wide[pl.ds(views_n, views_n), pl.ds(0, blocks_n)] = shifts_ref[...].astype(F32)
    meta_ref[...] = meta_wide[...].T[:blocks_n].reshape(meta_ref.shape)
    loads[2].wait()
    pl.semaphore_wait(barrier, gy_n)

    meta_copies = [
        send(meta_ref, meta_band.at[c, pl.ds(1, 2)], meta_s.at[k], meta_r.at[k], {"gy": p})
        for k, p in enumerate(peers)
    ]
    est_n = part_n + HALO
    gathers = []
    for k, p in enumerate(peers):
        layer, other = place_of(p)
        gathers.append(
            send(
                est_ref.at[layer, pl.ds(HALO * other, est_n)],
                est_band.at[0, c, pl.ds(HALO - HALO * other, est_n)],
                gather_s.at[k], gather_r.at[k], {"gy": p},
            )
        )
    loads[3].wait()
    for view in range(views_n):
        for layer in range(depth):
            views_out[view, layer] = (
                views_ref[view, layer].astype(F32).reshape(blocks_n, block_rows, width)
            )
    seen = pl.ds(NEAR, part_n)
    view_copies = []

    def send_view(view):
        copies = []
        for k, p in enumerate(peers):
            layer, other = place_of(p)
            copies.append(
                send(
                    views_out.at[view, layer, pl.ds(part_n * other, part_n)],
                    views_band.at[view, c, seen],
                    views_s.at[view, k], views_r.at[view, k], {"gy": p},
                )
            )
        view_copies.append(copies)

    send_view(0)
    meta_band[c, pl.ds(1, 2)] = meta_ref[...]
    est_band[0, c, pl.ds(HALO - HALO * h, est_n)] = est_ref[plane, pl.ds(HALO * h, est_n)]
    for view in range(views_n):
        views_band[view, c, seen] = views_out[view, plane, pl.ds(part_n * h, part_n)]

    for load in loads[4:]:
        load.wait()
    first_row = jnp.where((g == 0) & (h == 0), 0, -HALO * block_rows)
    last_row = jnp.where((g == gx_n - 1) & (h == 1), part_rows, part_rows + HALO * block_rows)
    for view in range(views_n):
        taps, total = taps_of(psf_rows_ref, view)
        row = lax.broadcasted_iota(jnp.int32, (near_rows, band_rows), 0) - NEAR * block_rows
        col = lax.broadcasted_iota(jnp.int32, (near_rows, band_rows), 1) - HALO * block_rows
        inside = (col >= first_row) & (col < last_row)
        outer = (row < first_row) | (row >= last_row)
        value = jnp.where(inside | outer, banded(taps, total, col - row + half), 0.0)
        store_halves(band_fwd.at[view], value)
        row = lax.broadcasted_iota(jnp.int32, (part_rows, near_rows), 0)
        col = lax.broadcasted_iota(jnp.int32, (part_rows, near_rows), 1) - NEAR * block_rows
        inside = (col >= first_row) & (col < last_row)
        value = jnp.where(inside, banded(taps, total, row - col + half), 0.0)
        store_halves(band_back.at[view], value)
        taps, total = taps_of(psf_cols_ref, view)
        for ref, sign in ((cols_fwd.at[view], 1), (cols_back.at[view], -1)):
            row = lax.broadcasted_iota(jnp.int32, (width, width), 0)
            col = lax.broadcasted_iota(jnp.int32, (width, width), 1)
            value = banded(taps, total, sign * (row - col) + half)
            store_terms(ref, 0, 0, 2 * width, value)
            store_terms(ref, width, width, 2 * width, value)
            row, col = row[:16], col[:16]
            blank = jnp.zeros((width - 16, width), F32)
            value = banded(taps, total, sign * (row + width - col) + half)
            value = jnp.concatenate([value, blank], axis=0)
            store_terms(ref, width, 0, 2 * width, value)
            value = banded(taps, total, sign * (row - 16 - col) + half)
            value = jnp.concatenate([blank, value], axis=0)
            store_terms(ref, 0, width, 2 * width, value)

    for copy in meta_copies:
        copy.wait_recv()
    edge = send(
        meta_band.at[:, 1 + h], meta_band.at[:, 3 - 3 * h], edge_s.at[0], edge_r.at[0], beside
    )
    for copy in gathers:
        copy.wait_recv()
    halo = send(
        est_band.at[0, :, pl.ds(HALO + (part_n - HALO) * h, HALO)],
        est_band.at[0, :, pl.ds((part_n + HALO) * (1 - h), HALO)],
        halo_s.at[0], halo_r.at[0], beside,
    )
    send_view(1)
    send_view(2)

    edge.wait_recv()
    for j in range(gy_n):
        found = meta_band[j].reshape(4 * 8, width)
        for view in range(views_n):
            lines[view, j] = jnp.broadcast_to(found[:, view : view + 1], found.shape)
            if j == 0:
                near = found[:, views_n + view : views_n + view + 1]
                lines[view, gy_n] = jnp.broadcast_to(near, found.shape)

    lane = lax.broadcasted_iota(jnp.int32, (block_rows, width), 1)

    def spread(b, carry):
        place = pl.ds(b + 8 - HALO + part_n * h, 1)
        for view in range(views_n):
            for j in range(gy_n):
                line = jnp.broadcast_to(lines[view, j, place, :], (block_rows, width))
                frac_full[view, j, b] = jnp.where(lane < width - 1, line, 0.0)
            shift_full[view, b] = jnp.broadcast_to(
                lines[view, gy_n, place, :], (block_rows, width)
            )
        return carry

    lax.fori_loop(0, part_n + 2 * HALO, spread, 0)
    halo.wait_recv()

    def pick(shift, tiles, first, sign):
        value = tiles[first % gy_n]
        for k in range(1, gy_n):
            value = jnp.where(shift == float(k), tiles[(first + sign * k) % gy_n], value)
        return value

    own = pl.ds(HALO, part_n)

    def viewed(sweep, view, start, count):
        place = pl.ds(start, count)
        rows = count * block_rows
        shift = shift_full[view, place]
        tiles = [est_band[sweep, j, place] for j in range(gy_n)]
        parts = []
        for j in range(gy_n):
            moved = pick(shift, tiles, j, 1).reshape(rows, width)
            fraction = frac_full[view, j, place].reshape(rows, width)
            following = pltpu.roll(moved, width - 1, 1)
            parts.append(moved + fraction * (following - moved))
        return jnp.concatenate(parts, axis=1)

    def blur(sweep, views):
        fields = [viewed(sweep, view, 0, part_n + 2 * HALO) for view in views]
        fields = [rows_by(band_fwd.at[view], x) for view, x in zip(views, fields)]
        return [cols_by(x, cols_fwd.at[view]) for view, x in zip(views, fields)]

    def blur_cols_first(sweep, views, halos):
        inner = [viewed(sweep, view, HALO, part_n) for view in views]
        inner = [cols_by(x, cols_fwd.at[view]) for view, x in zip(views, inner)]
        inner = [jnp.concatenate(tiles, axis=1) for tiles in inner]
        for copy in halos:
            copy.wait_recv()
        cut = HALO * block_rows
        outer = [
            jnp.concatenate(
                [viewed(sweep, view, 0, HALO), viewed(sweep, view, HALO + part_n, HALO)], axis=0
            )
            for view in views
        ]
        outer = [cols_by(x, cols_fwd.at[view]) for view, x in zip(views, outer)]
        outer = [jnp.concatenate(tiles, axis=1) for tiles in outer]
        fields = [jnp.concatenate([o[:cut], i, o[cut:]], axis=0) for i, o in zip(inner, outer)]
        fields = [rows_by(band_fwd.at[view], x) for view, x in zip(views, fields)]
        return [[x[:, j * width : (j + 1) * width] for j in range(gy_n)] for x in fields]

    def rows_back(views, blurred):
        ratio = [
            [views_band[view, j].reshape(near_rows, width) / tiles[j] for j in range(gy_n)]
            for view, tiles in zip(views, blurred)
        ]
        return [
            rows_by(band_back.at[view], jnp.concatenate(tiles, axis=1))
            for view, tiles in zip(views, ratio)
        ]

    def correct(views, fields, start, count):
        rows = count * block_rows
        place = pl.ds(HALO + start, count)
        fields = [x[start * block_rows : start * block_rows + rows] for x in fields]
        back = [cols_by(x, cols_back.at[view]) for view, x in zip(views, fields)]
        homes = []
        for view, tiles in zip(views, back):
            returned = []
            for j in range(gy_n):
                passed = frac_full[view, j, place].reshape(rows, width) * tiles[j]
                value = tiles[j] - passed + pltpu.roll(passed, 1, 1)
                returned.append(value.reshape(count, block_rows, width))
            shift = shift_full[view, place]
            homes.append([pick(shift, returned, j, -1) for j in range(gy_n)])
        return homes

    def add_up(all_homes):
        return functools.reduce(lambda x, y: [a + b for a, b in zip(x, y)], all_homes)

    def arrive(view):
        for copy in view_copies[view]:
            copy.wait_recv()
        band = views_band.at[view]
        nears = [
            send(
                band.at[:, pl.ds(part_n - (part_n - NEAR) * h, NEAR)],
                band.at[:, pl.ds((part_n + NEAR) * h, NEAR)],
                near_s.at[view, 0], near_r.at[view, 0], partner,
            ),
            send(
                band.at[:, pl.ds(NEAR + (part_n - NEAR) * h, NEAR)],
                band.at[:, pl.ds((part_n + NEAR) * (1 - h), NEAR)],
                near_s.at[view, 1], near_r.at[view, 1], beside,
            ),
        ]
        if view + 3 < views_n:
            send_view(view + 3)
        return nears

    every = list(range(views_n))
    for sweep in range(ITERS):
        if sweep == 0:
            blurred = blur(sweep, every)
            nears = [arrive(0), arrive(1)]
            homes = []
            for view in every:
                if len(nears) < min(view + 2, views_n):
                    nears.append(arrive(len(nears)))
                for copy in nears[view]:
                    copy.wait_recv()
                fields = rows_back([view], [blurred[view]])
                homes += correct([view], fields, 0, part_n)
        else:
            fields = rows_back(every, blur_cols_first(sweep, every, halos))
            if sweep + 1 < ITERS:
                homes = correct(every, fields, 0, part_n)
        if sweep + 1 < ITERS:
            sums = add_up(homes)
            for j in range(gy_n):
                est_band[sweep + 1, j, own] = est_band[sweep, j, own] * (sums[j] / views_n)
            band = est_band.at[sweep + 1]
            halos = [
                send(
                    band.at[:, pl.ds(part_n - (part_n - HALO) * h, HALO)],
                    band.at[:, pl.ds((part_n + HALO) * h, HALO)],
                    halo_s.at[2 * sweep + 1], halo_r.at[2 * sweep + 1], partner,
                ),
                send(
                    band.at[:, pl.ds(HALO + (part_n - HALO) * h, HALO)],
                    band.at[:, pl.ds((part_n + HALO) * (1 - h), HALO)],
                    halo_s.at[2 * sweep + 2], halo_r.at[2 * sweep + 2], beside,
                ),
            ]
    outs = []
    count = part_n // 2
    for piece in range(2):
        start = piece * count
        sums = add_up(correct(every, fields, start, count))
        for j in range(gy_n):
            joined = est_band[ITERS - 1, j, pl.ds(HALO + start, count)]
            out_own[piece, j] = joined * (sums[j] / views_n)
        place = pl.ds(part_n * h + start, count)
        outs += [
            send(
                out_own.at[piece, p], out_in.at[plane, place],
                out_s.at[piece, k], out_r.at[piece, k], {"gy": p},
            )
            for k, p in enumerate(peers)
        ]
        out_in[plane, place] = out_own[piece, c]
    for copy in outs:
        copy.wait_recv()
    out_ref[...] = out_in[...]
    for copy in pending:
        copy.wait_send()


def band_body(gx_n, gy_n, estimate, views, psf_rows, psf_cols, shifts, codes):
    views_n, depth, tile_rows, width = views.shape
    blocks_n = shifts.shape[1]
    block_rows = tile_rows // blocks_n
    part_n = blocks_n // 2
    part_rows = part_n * block_rows
    near_rows = part_rows + 2 * NEAR * block_rows
    band_rows = part_rows + 2 * HALO * block_rows
    others = gy_n - 1
    vmem = pltpu.VMEM
    dma = pltpu.SemaphoreType.DMA
    out = pl.pallas_call(
        functools.partial(kernel, gx_n, gy_n),
        out_shape=pltpu.VMEM((depth, blocks_n, block_rows, width), F32),
        in_specs=[pl.BlockSpec(memory_space=pltpu.HBM)] * 6,
        out_specs=pl.BlockSpec(memory_space=pltpu.VMEM),
        scratch_shapes=[
            vmem((depth, blocks_n, block_rows, width), F32),
            vmem(views.shape, BF16),
            vmem(shifts.shape, jnp.int32),
            vmem((views_n, blocks_n), jnp.int32),
            pltpu.SMEM(psf_rows.shape, F32),
            pltpu.SMEM(psf_cols.shape, F32),
            vmem((width, width), F32),
            vmem((2, 8, width), F32),
            vmem((ITERS, gy_n, part_n + 2 * HALO, block_rows, width), F32),
            vmem((views_n, depth, blocks_n, block_rows, width), F32),
            vmem((views_n, gy_n, part_n + 2 * NEAR, block_rows, width), F32),
            vmem((gy_n, 4, 8, width), F32),
            vmem((views_n, gy_n + 1, 4 * 8, width), F32),
            vmem((views_n, gy_n, part_n + 2 * HALO, block_rows, width), F32),
            vmem((views_n, part_n + 2 * HALO, block_rows, width), F32),
            vmem((2, gy_n, part_n // 2, block_rows, width), F32),
            vmem((depth, blocks_n, block_rows, width), F32),
            vmem((views_n, 2 * near_rows, 2 * band_rows), BF16),
            vmem((views_n, 2 * part_rows, 2 * near_rows), BF16),
            vmem((views_n, 6 * width, 2 * width), BF16),
            vmem((views_n, 6 * width, 2 * width), BF16),
            dma((6,)),
            dma((others,)), dma((others,)),
            dma((2 * ITERS - 1,)), dma((2 * ITERS - 1,)),
            dma((views_n, others)), dma((views_n, others)),
            dma((views_n, 2)), dma((views_n, 2)),
            dma((others,)), dma((others,)),
            dma((1,)), dma((1,)),
            dma((2, others)), dma((2, others)),
        ],
        compiler_params=pltpu.CompilerParams(
            collective_id=0, has_side_effects=True, vmem_limit_bytes=56 * 1024 * 1024
        ),
    )(
        estimate.reshape(depth, blocks_n, block_rows, width), views, shifts,
        codes.reshape(views_n, blocks_n), psf_rows, psf_cols,
    )
    return out.reshape(depth, tile_rows, width)


def solution(mesh):
    placed = (
        P(None, "gx", "gy"),
        P(None, None, "gx", "gy"),
        P(),
        P(),
        P(None, "gx"),
        P(None, "gx", "gy"),
    )
    gx_n, gy_n = mesh.shape["gx"], mesh.shape["gy"]

    def body(estimate, views, *rest):
        parts_n = 2 * estimate.shape[0]
        if gy_n == parts_n and gx_n % 2 == 0 and rest[2].shape[1] == 16:
            return band_body(gx_n, gy_n, estimate, views, *rest)
        return tile_body(estimate, views, *rest)

    return jax.shard_map(
        body, mesh=mesh, in_specs=placed, out_specs=P(None, "gx", "gy"), check_vma=False
    )
```

```python
import functools

import jax
import jax.numpy as jnp
from jax import lax
from jax.experimental import pallas as pl
from jax.experimental.pallas import tpu as pltpu
from jax.sharding import PartitionSpec as P

ITERS = 2
MESH = pl.DeviceIdType.MESH
F32 = jnp.float32
BF16 = jnp.bfloat16
HALO = 4
NEAR = 2


def with_halo(block, sides, width):
    for axis, dim in sides:
        count = lax.axis_size(axis)
        forward = [(i, i + 1) for i in range(count - 1)]
        backward = [(target, source) for source, target in forward]
        low = lax.ppermute(
            lax.slice_in_dim(block, block.shape[dim] - width, None, axis=dim), axis, forward
        )
        high = lax.ppermute(lax.slice_in_dim(block, 0, width, axis=dim), axis, backward)
        block = jnp.concatenate([low, block, high], axis=dim)
    return block


def shift_in(values, fraction):
    last = values.shape[-1] - 1
    column = lax.broadcasted_iota(jnp.int32, values.shape, values.ndim - 1)
    following = jnp.concatenate([values[..., 1:], values[..., -1:]], axis=-1)
    return jnp.where(column < last, (1.0 - fraction) * values + fraction * following, values)


def shift_back(values, fraction):
    last = values.shape[-1] - 1
    column = lax.broadcasted_iota(jnp.int32, values.shape, values.ndim - 1)
    preceding = jnp.concatenate([jnp.zeros_like(values[..., :1]), values[..., :-1]], axis=-1)
    own_part = jnp.where(column < last, (1.0 - fraction) * values, values)
    return own_part + fraction * preceding


def smooth_rows(padded, taps, count):
    total = taps[0] * padded[..., 0:count, :]
    for offset in range(1, taps.shape[0]):
        total = total + taps[offset] * padded[..., offset : offset + count, :]
    return total


def smooth_cols(padded, taps, count):
    total = taps[0] * padded[..., 0:count]
    for offset in range(1, taps.shape[0]):
        total = total + taps[offset] * padded[..., offset : offset + count]
    return total


def tile_body(estimate, views, psf_rows, psf_cols, shifts, codes):
    highest = lax.Precision.HIGHEST
    groups = lax.axis_size("gy")
    column = lax.axis_index("gy")
    views_n, depth, tile_rows, tile_cols = views.shape
    blocks_n = shifts.shape[1]
    block_rows = tile_rows // blocks_n
    capacity = 1 + (blocks_n + groups - 2) // groups
    tap_count = psf_rows.shape[1]
    half = tap_count // 2
    kern_rows = psf_rows / jnp.sum(psf_rows, axis=1, keepdims=True)
    kern_cols = psf_cols / jnp.sum(psf_cols, axis=1, keepdims=True)
    taps_rows = kern_rows.T.reshape(tap_count, views_n, 1, 1, 1)
    taps_cols = kern_cols.T.reshape(tap_count, views_n, 1, 1, 1)
    flipped_rows = kern_rows[:, ::-1].T.reshape(tap_count, views_n, 1, 1, 1)
    flipped_cols = kern_cols[:, ::-1].T.reshape(tap_count, views_n, 1, 1, 1)
    fraction = (codes[:, :, 0].astype(jnp.float32) / 16.0)[:, None, :, None, None]
    block_ids = jnp.arange(blocks_n, dtype=jnp.int32)
    same_shift = shifts[:, :, None] == shifts[:, None, :]
    earlier = block_ids[None, None, :] < block_ids[None, :, None]
    slot_rank = jnp.sum((same_shift & earlier).astype(jnp.int32), axis=2)
    peer_ids = jnp.arange(groups, dtype=jnp.int32)
    slot_ids = jnp.arange(capacity, dtype=jnp.int32)
    source_peer = (column + shifts) % groups
    target_peer = (column - shifts) % groups
    send_hot = (
        (peer_ids[None, :, None, None] == target_peer[:, None, None, :])
        & (slot_ids[None, None, :, None] == slot_rank[:, None, None, :])
    ).astype(jnp.float32)
    recv_hot = (
        (peer_ids[None, None, :, None] == source_peer[:, :, None, None])
        & (slot_ids[None, None, None, :] == slot_rank[:, :, None, None])
    ).astype(jnp.float32)
    for sweep in range(ITERS):
        blocked = estimate.reshape(depth, blocks_n, block_rows, tile_cols)
        outgoing = jnp.einsum("vpqk,zkrw->pvqzrw", send_hot, blocked, precision=highest)
        arriving = lax.all_to_all(outgoing, "gy", split_axis=0, concat_axis=0, tiled=True)
        view_blocks = jnp.einsum("vkpq,pvqzrw->vzkrw", recv_hot, arriving, precision=highest)
        view_est = shift_in(view_blocks, fraction).reshape(views_n, depth, tile_rows, tile_cols)
        padded = with_halo(view_est, (("gx", 2), ("gy", 3)), half)
        rows_done = smooth_rows(padded, taps_rows, tile_rows)
        blurred = smooth_cols(rows_done, taps_cols, tile_cols)
        ratio = views.astype(jnp.float32) / blurred
        padded_ratio = with_halo(ratio, (("gx", 2), ("gy", 3)), half)
        rows_back = smooth_rows(padded_ratio, flipped_rows, tile_rows)
        back = smooth_cols(rows_back, flipped_cols, tile_cols)
        returned = shift_back(
            back.reshape(views_n, depth, blocks_n, block_rows, tile_cols), fraction
        )
        leaving = jnp.einsum("vkpq,vzkrw->pvqzrw", recv_hot, returned, precision=highest)
        coming = lax.all_to_all(leaving, "gy", split_axis=0, concat_axis=0, tiled=True)
        summed = jnp.einsum("vpqk,pvqzrw->zkrw", send_hot, coming, precision=highest)
        estimate = estimate * (summed.reshape(depth, tile_rows, tile_cols) / views_n)
    return estimate


def split(value):
    high = value.astype(BF16)
    return high, (value - high.astype(F32)).astype(BF16)


def store_terms(ref, rows, cols, step, value):
    high, low = split(value)
    for k, part in enumerate((high, high, low)):
        ref[pl.ds(rows + k * step, value.shape[0]), pl.ds(cols, value.shape[1])] = part


def terms(value):
    high, low = split(value)
    return jnp.concatenate([high, low, high], axis=1)


def product(left, right):
    return lax.dot_general(left, right, (((1,), (0,)), ((), ())), preferred_element_type=F32)


def store_halves(ref, value):
    rows, cols = value.shape
    for k, part in enumerate(split(value)):
        for j in range(2):
            ref[pl.ds(k * rows, rows), pl.ds(j * cols, cols)] = part


def rows_by(band, field):
    done = product(band[...], jnp.concatenate(split(field), axis=0))
    rows = done.shape[0] // 2
    return done[:rows] + done[rows:]


def cols_by(field, band):
    width = band.shape[1] // 2
    rows = field.shape[0]
    count = field.shape[1] // width - 1
    windows = [field[:, j * width : (j + 2) * width] for j in range(count)]
    done = product(terms(jnp.concatenate(windows, axis=0)), band[...])
    done = [done[j * rows : (j + 1) * rows] for j in range(count)]
    lane = lax.broadcasted_iota(jnp.int32, (rows, width), 1)
    tiles = [done[0][:, :width]]
    for j in range(count - 1):
        tiles.append(jnp.where(lane < width // 2, done[j][:, width:], done[j + 1][:, :width]))
    tiles.append(done[-1][:, width:])
    return tiles


def taps_of(ref, view):
    taps = [ref[view, t] for t in range(ref.shape[1])]
    return taps, functools.reduce(lambda a, b: a + b, taps)


def banded(taps, total, offset):
    value = jnp.zeros(offset.shape, F32)
    for t, tap in enumerate(taps):
        value = jnp.where(offset == t, tap, value)
    return value / jnp.full(offset.shape, total, F32)


def kernel(
    gx_n, gy_n, est_hbm, views_hbm, shifts_hbm, codes_hbm, psf_rows_hbm, psf_cols_hbm, out_ref,
    est_ref, views_ref, shifts_ref, codes_ref, psf_rows_ref, psf_cols_ref, meta_wide, meta_ref,
    est_band, views_out, views_band, meta_band, lines, frac_full, shift_full, out_own, out_in,
    band_fwd, band_back, cols_fwd, cols_back,
    local, gather_s, gather_r, halo_s, halo_r, views_s, views_r, near_s, near_r,
    meta_s, meta_r, edge_s, edge_r, out_s, out_r,
):
    views_n, depth, _, width = views_ref.shape
    blocks_n, block_rows = est_ref.shape[1:3]
    part_n = blocks_n // 2
    part_rows = part_n * block_rows
    band_rows = (part_n + 2 * HALO) * block_rows
    near_rows = (part_n + 2 * NEAR) * block_rows
    half = psf_rows_ref.shape[1] // 2
    g = lax.axis_index("gx")
    c = lax.axis_index("gy")

    def place_of(device):
        return device // 2, lax.rem(device + g, 2)

    plane, h = place_of(c)
    peers = [lax.rem(c + k, gy_n) for k in range(1, gy_n)]
    partner = {"gy": c + 1 - 2 * lax.rem(c, 2)}
    beside = {"gx": lax.rem(g - 1 + 2 * h + gx_n, gx_n)}
    pending = []

    def send(src, dst, send_sem, recv_sem, target):
        copy = pltpu.make_async_remote_copy(
            src_ref=src, dst_ref=dst, send_sem=send_sem, recv_sem=recv_sem,
            device_id=target, device_id_type=MESH,
        )
        copy.start()
        pending.append(copy)
        return copy

    loads = [
        pltpu.make_async_copy(src, dst, local.at[k])
        for k, (src, dst) in enumerate(
            (
                (codes_hbm, codes_ref), (shifts_hbm, shifts_ref), (est_hbm, est_ref),
                (views_hbm, views_ref), (psf_rows_hbm, psf_rows_ref), (psf_cols_hbm, psf_cols_ref),
            )
        )
    ]
    for load in loads:
        load.start()
    barrier = pltpu.get_barrier_semaphore()
    for target in [{"gy": p} for p in peers] + [beside]:
        pl.semaphore_signal(barrier, inc=1, device_id=target, device_id_type=MESH)
    meta_wide[...] = jnp.zeros(meta_wide.shape, F32)
    for load in loads[:2]:
        load.wait()
    meta_wide[pl.ds(0, views_n), pl.ds(0, blocks_n)] = codes_ref[...].astype(F32) / 16.0
    meta_wide[pl.ds(views_n, views_n), pl.ds(0, blocks_n)] = shifts_ref[...].astype(F32)
    meta_ref[...] = meta_wide[...].T[:blocks_n].reshape(meta_ref.shape)
    loads[2].wait()
    pl.semaphore_wait(barrier, gy_n)

    meta_copies = [
        send(meta_ref, meta_band.at[c, pl.ds(1, 2)], meta_s.at[k], meta_r.at[k], {"gy": p})
        for k, p in enumerate(peers)
    ]
    est_n = part_n + HALO
    gathers = []
    for k, p in enumerate(peers):
        layer, other = place_of(p)
        gathers.append(
            send(
                est_ref.at[layer, pl.ds(HALO * other, est_n)],
                est_band.at[0, c, pl.ds(HALO - HALO * other, est_n)],
                gather_s.at[k], gather_r.at[k], {"gy": p},
            )
        )
    loads[3].wait()
    for view in range(views_n):
        for layer in range(depth):
            views_out[view, layer] = (
                views_ref[view, layer].astype(F32).reshape(blocks_n, block_rows, width)
            )
    seen = pl.ds(NEAR, part_n)
    view_copies = []

    def send_view(view):
        copies = []
        for k, p in enumerate(peers):
            layer, other = place_of(p)
            copies.append(
                send(
                    views_out.at[view, layer, pl.ds(part_n * other, part_n)],
                    views_band.at[view, c, seen],
                    views_s.at[view, k], views_r.at[view, k], {"gy": p},
                )
            )
        view_copies.append(copies)

    send_view(0)
    meta_band[c, pl.ds(1, 2)] = meta_ref[...]
    est_band[0, c, pl.ds(HALO - HALO * h, est_n)] = est_ref[plane, pl.ds(HALO * h, est_n)]
    for view in range(views_n):
        views_band[view, c, seen] = views_out[view, plane, pl.ds(part_n * h, part_n)]

    for load in loads[4:]:
        load.wait()
    first_row = jnp.where((g == 0) & (h == 0), 0, -HALO * block_rows)
    last_row = jnp.where((g == gx_n - 1) & (h == 1), part_rows, part_rows + HALO * block_rows)
    for view in range(views_n):
        taps, total = taps_of(psf_rows_ref, view)
        row = lax.broadcasted_iota(jnp.int32, (near_rows, band_rows), 0) - NEAR * block_rows
        col = lax.broadcasted_iota(jnp.int32, (near_rows, band_rows), 1) - HALO * block_rows
        inside = (col >= first_row) & (col < last_row)
        outer = (row < first_row) | (row >= last_row)
        value = jnp.where(inside | outer, banded(taps, total, col - row + half), 0.0)
        store_halves(band_fwd.at[view], value)
        row = lax.broadcasted_iota(jnp.int32, (part_rows, near_rows), 0)
        col = lax.broadcasted_iota(jnp.int32, (part_rows, near_rows), 1) - NEAR * block_rows
        inside = (col >= first_row) & (col < last_row)
        value = jnp.where(inside, banded(taps, total, row - col + half), 0.0)
        store_halves(band_back.at[view], value)
        taps, total = taps_of(psf_cols_ref, view)
        for ref, sign in ((cols_fwd.at[view], 1), (cols_back.at[view], -1)):
            row = lax.broadcasted_iota(jnp.int32, (width, width), 0)
            col = lax.broadcasted_iota(jnp.int32, (width, width), 1)
            value = banded(taps, total, sign * (row - col) + half)
            store_terms(ref, 0, 0, 2 * width, value)
            store_terms(ref, width, width, 2 * width, value)
            row, col = row[:16], col[:16]
            blank = jnp.zeros((width - 16, width), F32)
            value = banded(taps, total, sign * (row + width - col) + half)
            value = jnp.concatenate([value, blank], axis=0)
            store_terms(ref, width, 0, 2 * width, value)
            value = banded(taps, total, sign * (row - 16 - col) + half)
            value = jnp.concatenate([blank, value], axis=0)
            store_terms(ref, 0, width, 2 * width, value)

    for copy in meta_copies:
        copy.wait_recv()
    edge = send(
        meta_band.at[:, 1 + h], meta_band.at[:, 3 - 3 * h], edge_s.at[0], edge_r.at[0], beside
    )
    for copy in gathers:
        copy.wait_recv()
    halo = send(
        est_band.at[0, :, pl.ds(HALO + (part_n - HALO) * h, HALO)],
        est_band.at[0, :, pl.ds((part_n + HALO) * (1 - h), HALO)],
        halo_s.at[0], halo_r.at[0], beside,
    )
    for view in range(1, views_n):
        send_view(view)

    edge.wait_recv()
    for j in range(gy_n):
        found = meta_band[j].reshape(4 * 8, width)
        for view in range(views_n):
            lines[view, j] = jnp.broadcast_to(found[:, view : view + 1], found.shape)
            if j == 0:
                near = found[:, views_n + view : views_n + view + 1]
                lines[view, gy_n] = jnp.broadcast_to(near, found.shape)

    lane = lax.broadcasted_iota(jnp.int32, (block_rows, width), 1)

    def spread(b, carry):
        place = pl.ds(b + 8 - HALO + part_n * h, 1)
        for view in range(views_n):
            for j in range(gy_n):
                line = jnp.broadcast_to(lines[view, j, place, :], (block_rows, width))
                frac_full[view, j, b] = jnp.where(lane < width - 1, line, 0.0)
            shift_full[view, b] = jnp.broadcast_to(
                lines[view, gy_n, place, :], (block_rows, width)
            )
        return carry

    lax.fori_loop(0, part_n + 2 * HALO, spread, 0)
    halo.wait_recv()

    def pick(shift, tiles, first, sign):
        value = tiles[first % gy_n]
        for k in range(1, gy_n):
            value = jnp.where(shift == float(k), tiles[(first + sign * k) % gy_n], value)
        return value

    own = pl.ds(HALO, part_n)

    def viewed(sweep, view, start, count):
        place = pl.ds(start, count)
        rows = count * block_rows
        shift = shift_full[view, place]
        tiles = [est_band[sweep, j, place] for j in range(gy_n)]
        parts = []
        for j in range(gy_n):
            moved = pick(shift, tiles, j, 1).reshape(rows, width)
            fraction = frac_full[view, j, place].reshape(rows, width)
            following = pltpu.roll(moved, width - 1, 1)
            parts.append(moved + fraction * (following - moved))
        return jnp.concatenate(parts, axis=1)

    def blur(sweep, views):
        fields = [viewed(sweep, view, 0, part_n + 2 * HALO) for view in views]
        fields = [rows_by(band_fwd.at[view], x) for view, x in zip(views, fields)]
        return [cols_by(x, cols_fwd.at[view]) for view, x in zip(views, fields)]

    def blur_cols_first(sweep, views, halos):
        inner = [viewed(sweep, view, HALO, part_n) for view in views]
        inner = [cols_by(x, cols_fwd.at[view]) for view, x in zip(views, inner)]
        inner = [jnp.concatenate(tiles, axis=1) for tiles in inner]
        for copy in halos:
            copy.wait_recv()
        cut = HALO * block_rows
        outer = [
            jnp.concatenate(
                [viewed(sweep, view, 0, HALO), viewed(sweep, view, HALO + part_n, HALO)], axis=0
            )
            for view in views
        ]
        outer = [cols_by(x, cols_fwd.at[view]) for view, x in zip(views, outer)]
        outer = [jnp.concatenate(tiles, axis=1) for tiles in outer]
        fields = [jnp.concatenate([o[:cut], i, o[cut:]], axis=0) for i, o in zip(inner, outer)]
        fields = [rows_by(band_fwd.at[view], x) for view, x in zip(views, fields)]
        return [[x[:, j * width : (j + 1) * width] for j in range(gy_n)] for x in fields]

    def correct(views, blurred):
        ratio = [
            [views_band[view, j].reshape(near_rows, width) / tiles[j] for j in range(gy_n)]
            for view, tiles in zip(views, blurred)
        ]
        fields = [
            rows_by(band_back.at[view], jnp.concatenate(tiles, axis=1))
            for view, tiles in zip(views, ratio)
        ]
        back = [cols_by(x, cols_back.at[view]) for view, x in zip(views, fields)]
        homes = []
        for view, tiles in zip(views, back):
            returned = []
            for j in range(gy_n):
                passed = frac_full[view, j, own].reshape(part_rows, width) * tiles[j]
                value = tiles[j] - passed + pltpu.roll(passed, 1, 1)
                returned.append(value.reshape(part_n, block_rows, width))
            shift = shift_full[view, own]
            homes.append([pick(shift, returned, j, -1) for j in range(gy_n)])
        return homes

    def add_up(all_homes):
        return functools.reduce(lambda x, y: [a + b for a, b in zip(x, y)], all_homes)

    def arrive(view):
        for copy in view_copies[view]:
            copy.wait_recv()
        band = views_band.at[view]
        nears = [
            send(
                band.at[:, pl.ds(part_n - (part_n - NEAR) * h, NEAR)],
                band.at[:, pl.ds((part_n + NEAR) * h, NEAR)],
                near_s.at[view, 0], near_r.at[view, 0], partner,
            ),
            send(
                band.at[:, pl.ds(NEAR + (part_n - NEAR) * h, NEAR)],
                band.at[:, pl.ds((part_n + NEAR) * (1 - h), NEAR)],
                near_s.at[view, 1], near_r.at[view, 1], beside,
            ),
        ]
        return nears

    for sweep in range(ITERS):
        if sweep == 0:
            nears = []
            blurred = []
            for view in range(0, views_n, 2):
                blurred += blur(sweep, list(range(view, min(view + 2, views_n))))
                nears.append(arrive(view // 2))
            homes = []
            for view in range(views_n):
                if len(nears) < min(view + 2, views_n):
                    nears.append(arrive(len(nears)))
                for copy in nears[view]:
                    copy.wait_recv()
                homes += correct([view], [blurred[view]])
        else:
            every = list(range(views_n))
            homes = correct(every, blur_cols_first(sweep, every, halos))
        sums = add_up(homes)
        updated = [est_band[sweep, j, own] * (sums[j] / views_n) for j in range(gy_n)]
        if sweep + 1 < ITERS:
            for j in range(gy_n):
                est_band[sweep + 1, j, own] = updated[j]
            band = est_band.at[sweep + 1]
            halos = [
                send(
                    band.at[:, pl.ds(part_n - (part_n - HALO) * h, HALO)],
                    band.at[:, pl.ds((part_n + HALO) * h, HALO)],
                    halo_s.at[2 * sweep + 1], halo_r.at[2 * sweep + 1], partner,
                ),
                send(
                    band.at[:, pl.ds(HALO + (part_n - HALO) * h, HALO)],
                    band.at[:, pl.ds((part_n + HALO) * (1 - h), HALO)],
                    halo_s.at[2 * sweep + 2], halo_r.at[2 * sweep + 2], beside,
                ),
            ]
    for j in range(gy_n):
        out_own[j] = updated[j]
    place = pl.ds(part_n * h, part_n)
    outs = [
        send(out_own.at[p], out_in.at[plane, place], out_s.at[k], out_r.at[k], {"gy": p})
        for k, p in enumerate(peers)
    ]
    out_in[plane, place] = out_own[c]
    for copy in outs:
        copy.wait_recv()
    out_ref[...] = out_in[...]
    for copy in pending:
        copy.wait_send()


def band_body(gx_n, gy_n, estimate, views, psf_rows, psf_cols, shifts, codes):
    views_n, depth, tile_rows, width = views.shape
    blocks_n = shifts.shape[1]
    block_rows = tile_rows // blocks_n
    part_n = blocks_n // 2
    part_rows = part_n * block_rows
    near_rows = part_rows + 2 * NEAR * block_rows
    band_rows = part_rows + 2 * HALO * block_rows
    others = gy_n - 1
    vmem = pltpu.VMEM
    dma = pltpu.SemaphoreType.DMA
    out = pl.pallas_call(
        functools.partial(kernel, gx_n, gy_n),
        out_shape=pltpu.VMEM((depth, blocks_n, block_rows, width), F32),
        in_specs=[pl.BlockSpec(memory_space=pltpu.HBM)] * 6,
        out_specs=pl.BlockSpec(memory_space=pltpu.VMEM),
        scratch_shapes=[
            vmem((depth, blocks_n, block_rows, width), F32),
            vmem(views.shape, BF16),
            vmem(shifts.shape, jnp.int32),
            vmem((views_n, blocks_n), jnp.int32),
            pltpu.SMEM(psf_rows.shape, F32),
            pltpu.SMEM(psf_cols.shape, F32),
            vmem((width, width), F32),
            vmem((2, 8, width), F32),
            vmem((ITERS, gy_n, part_n + 2 * HALO, block_rows, width), F32),
            vmem((views_n, depth, blocks_n, block_rows, width), F32),
            vmem((views_n, gy_n, part_n + 2 * NEAR, block_rows, width), F32),
            vmem((gy_n, 4, 8, width), F32),
            vmem((views_n, gy_n + 1, 4 * 8, width), F32),
            vmem((views_n, gy_n, part_n + 2 * HALO, block_rows, width), F32),
            vmem((views_n, part_n + 2 * HALO, block_rows, width), F32),
            vmem((gy_n, part_n, block_rows, width), F32),
            vmem((depth, blocks_n, block_rows, width), F32),
            vmem((views_n, 2 * near_rows, 2 * band_rows), BF16),
            vmem((views_n, 2 * part_rows, 2 * near_rows), BF16),
            vmem((views_n, 6 * width, 2 * width), BF16),
            vmem((views_n, 6 * width, 2 * width), BF16),
            dma((6,)),
            dma((others,)), dma((others,)),
            dma((2 * ITERS - 1,)), dma((2 * ITERS - 1,)),
            dma((views_n, others)), dma((views_n, others)),
            dma((views_n, 2)), dma((views_n, 2)),
            dma((others,)), dma((others,)),
            dma((1,)), dma((1,)),
            dma((others,)), dma((others,)),
        ],
        compiler_params=pltpu.CompilerParams(
            collective_id=0, has_side_effects=True, vmem_limit_bytes=56 * 1024 * 1024
        ),
    )(
        estimate.reshape(depth, blocks_n, block_rows, width), views, shifts,
        codes.reshape(views_n, blocks_n), psf_rows, psf_cols,
    )
    return out.reshape(depth, tile_rows, width)


def solution(mesh):
    placed = (
        P(None, "gx", "gy"),
        P(None, None, "gx", "gy"),
        P(),
        P(),
        P(None, "gx"),
        P(None, "gx", "gy"),
    )
    gx_n, gy_n = mesh.shape["gx"], mesh.shape["gy"]

    def body(estimate, views, *rest):
        parts_n = 2 * estimate.shape[0]
        if gy_n == parts_n and gx_n % 2 == 0 and rest[2].shape[1] == 16:
            return band_body(gx_n, gy_n, estimate, views, *rest)
        return tile_body(estimate, views, *rest)

    return jax.shard_map(
        body, mesh=mesh, in_specs=placed, out_specs=P(None, "gx", "gy"), check_vma=False
    )
```
